256 devices in a mesh: member: 64 (over z, x, core), dp: 4 (over y).
Axes of the slice: x: 4, y: 4, z: 8, core: 2. Of those that a mesh axis runs over, the one named last changes fastest.
Arguments:
- feature_pool: bfloat16 [2048, 256], P('dp'), may hold values from -6 to 6
- labels: int32 [2048], P('dp'), may hold values from 0 to 9
- sample_rows: int32 [1024], P('dp'), may hold values from 0 to 511
- noise_variance: float32 [10], replicated, may hold values from 20 to 80
- first_weight: bfloat16 [128, 256, 2048], P('member', None, 'dp'), may hold values from -6 to 6
- middle_weight: bfloat16 [128, 2048, 2048], P('member', 'dp'), may hold values from -6 to 6
- last_weight: bfloat16 [128, 2048, 10], P('member', 'dp'), may hold values from -6 to 6
Outputs:
- new_first: bfloat16 [128, 256, 2048], P('member', None, 'dp')
- new_middle: bfloat16 [128, 2048, 2048], P('member', 'dp')
- new_last: bfloat16 [128, 2048, 10], P('member', 'dp')
The draws below stay inside these ranges and needn't reach their ends.
Inputs may be any that keep to these rules, and one draw needn't show every extreme that they name: Sample i reads pool row (i // 256) * 512 + sample_rows[i]. `labels`: class index of each pool row.
All inputs are finite; a program needn't handle non-finite values.
Results may differ from the reference program's by a relative error of at most 0.013.
Values may be sent and summed in bfloat16 or wider, within the bound.
A program may use at most 128 MiB of HBM per device.

```python
import math
import jax
import jax.numpy as jnp
from jax import lax

F_IN = 256
H = 2048
C = 10
SAMP_DEV = 256
POOL_DEV = 512
MEMBERS = 128
SAMPLES = 1024
POOL = 2048


def plant(array, own_key, low, top_value):
    longest = array.shape.index(max(array.shape))
    spots = []
    for shift in (0, 1):
        where = [jax.random.randint(jax.random.fold_in(own_key, axis), (), 0, length) for axis, length in enumerate(array.shape)]
        where[longest] = (where[longest] + shift) % array.shape[longest]
        spots.append(tuple(where))
    return array.at[spots[0]].set(low).at[spots[1]].set(top_value)


def steps_of(own_key, dims, shards, least, high):
    def one(dim, parts):
        steps = jax.random.uniform(jax.random.fold_in(jax.random.fold_in(own_key, 6), dim), (parts,), jnp.float32, least / len(shards), high / len(shards))
        return jnp.repeat(jnp.exp(steps), dims[dim] // parts).reshape((-1,) + (1,) * (len(dims) - dim - 1))

    gain = one(*shards[0])
    for cut in shards[1:]:
        gain = gain * one(*cut)
    return gain


def scatter_about(rng, shape, scale, bound, pieces=(), kind=jnp.bfloat16):
    drawn = scale * jax.random.normal(rng, shape, jnp.float32)
    if pieces:
        drawn = drawn * steps_of(rng, shape, pieces, -0.22, 0.18)
    return jnp.clip(drawn, -bound, bound).astype(kind)


def setup_inputs(seed: int = 0) -> dict:
    streams_of = jax.random.split(jax.random.key(seed), 8)
    return {
        "feature_pool": scatter_about(streams_of[0], (POOL, F_IN), 1.0, 6.0, ((0, 4),)),
        "labels": plant(jax.random.randint(streams_of[1], (POOL,), 0, C), jax.random.fold_in(streams_of[1], 1), 0, C - 1).astype(jnp.int32),
        "sample_rows": plant(jax.random.randint(streams_of[2], (SAMPLES,), 0, POOL_DEV), jax.random.fold_in(streams_of[2], 1), 0, POOL_DEV - 1).astype(jnp.int32),
        "noise_variance": jnp.clip(jnp.exp(jax.random.uniform(streams_of[3], (C,), jnp.float32, math.log(20.0), math.log(80.0))), 20.0, 80.0),
        "first_weight": scatter_about(streams_of[4], (MEMBERS, F_IN, H), 1.0, 6.0, ((0, 64), (2, 4))),
        "middle_weight": scatter_about(streams_of[5], (MEMBERS, H, H), 1.0, 6.0, ((0, 64), (1, 4))),
        "last_weight": scatter_about(streams_of[6], (MEMBERS, H, C), 1.0, 6.0, ((0, 64), (1, 4))),
    }


precise = lax.Precision.HIGHEST

def member_outputs(inputs, first, middle, last):
    hidden_one = jnp.tanh(jnp.dot(inputs.astype(jnp.float32), first.astype(jnp.float32), preferred_element_type=jnp.float32) * F_IN ** (-0.5)).astype(jnp.bfloat16)
    hidden_two = jnp.tanh(jnp.dot(hidden_one.astype(jnp.float32), middle.astype(jnp.float32), preferred_element_type=jnp.float32) * H ** (-0.5)).astype(jnp.bfloat16)
    return jnp.dot(hidden_two.astype(jnp.float32), last.astype(jnp.float32), preferred_element_type=jnp.float32) * H ** (-0.5)

def update_block(block, mixing):
    values = block.astype(jnp.float32)
    anomaly = values - lax.optimization_barrier(jnp.mean(values, axis=0, keepdims=True))
    return (values + jnp.dot(mixing.T, anomaly, precision=precise)).astype(jnp.bfloat16)

def update_tensor(tensor, mixing):
    moved = jnp.moveaxis(tensor, 1, 0)

    def one_row(block):
        return update_block(block, mixing)
    done = lax.map(one_row, moved)
    return jnp.moveaxis(done, 0, 1)

def reference(feature_pool, labels, sample_rows, noise_variance, first_weight, middle_weight, last_weight):
    positions = jnp.arange(SAMPLES, dtype=jnp.int32)
    rows = (positions // SAMP_DEV * POOL_DEV + sample_rows).astype(jnp.int32)
    inputs = feature_pool[rows]
    classes = labels[rows]
    target = (classes[:, None] == jnp.arange(C, dtype=jnp.int32)[None, :]).astype(jnp.float32)
    whiten = 1.0 / jnp.sqrt(noise_variance)

    def forward(weights):
        return member_outputs(inputs, weights[0], weights[1], weights[2])
    outputs = lax.map(forward, (first_weight, middle_weight, last_weight))
    scaled = (outputs * whiten).reshape(MEMBERS, SAMPLES * C)
    observed = (target * whiten).reshape(SAMPLES * C)
    center = lax.optimization_barrier(jnp.mean(scaled, axis=0))
    anomaly = scaled - center
    gram_matrix = jnp.dot(anomaly, anomaly.T, precision=precise)
    drive = jnp.dot(anomaly, observed - center, precision=precise)
    system = gram_matrix + MEMBERS * jnp.eye(MEMBERS, dtype=jnp.float32)
    factor = jnp.linalg.cholesky(system)
    mixing = jax.scipy.linalg.cho_solve((factor, True), drive[:, None] - gram_matrix)
    return (update_tensor(first_weight, mixing), update_tensor(middle_weight, mixing), update_tensor(last_weight, mixing))
```

```python
import functools

import jax
import jax.numpy as jnp
from jax import lax
from jax.experimental import pallas as pl
from jax.experimental.pallas import tpu as pltpu
from jax.sharding import PartitionSpec as P

F_IN = 256
H = 2048
MESH = pl.DeviceIdType.MESH
NM = 64
ND = 4
ENS = 128
TILE = 16
WIDE = 1024
SLIM = 128
LAST_TILES = 3
ROWS = 24
LAST_OWNERS = (3, 28, 53)
VMEM_LIMIT = 60 * 1024 * 1024


def middle_block(p):
    return pl.ds(pl.multiple_of((p // 2) * TILE, TILE), TILE), pl.ds(pl.multiple_of((p % 2) * WIDE, WIDE), WIDE)


def first_block(p):
    return pl.ds(pl.multiple_of((p // 4) * TILE, TILE), TILE), pl.ds(pl.multiple_of((p % 4) * SLIM, SLIM), SLIM)


def pair(p):
    return pl.ds(pl.multiple_of(2 * p, 2), 2)


def plane_peer(me, step):
    z, low = me // 8, me % 8
    plane, within = step // 8, step % 8
    return ((z + plane) % 8) * 8 + (low + within) % 8


def spd_inverse(system):
    size = system.shape[0]
    group = 8
    sub = lax.broadcasted_iota(jnp.int32, (group, size), 0)
    lane = lax.broadcasted_iota(jnp.int32, (group, size), 1)
    lanes = lax.broadcasted_iota(jnp.int32, (size - group, size), 1)

    def one_round(_, a):
        panel = a[:group, :]
        for k in range(group):
            row = panel[k:k + 1, :]
            col = panel[:, k:k + 1]
            pivot = 1.0 / row[:, k:k + 1]
            row = jnp.where(lane[:1] == k, pivot, row * pivot)
            panel = jnp.where(sub == k, row, jnp.where(lane == k, 0.0, panel) - col * row)
        below = jnp.where(lanes < group, 0.0, a[group:, :])
        for k in range(group):
            below = below - a[group:, k:k + 1] * panel[k:k + 1, :]
        turned = jnp.concatenate([below, panel], axis=0)
        return pltpu.roll(turned, size - group, 1)

    return lax.fori_loop(0, size // group, one_round, system)


def member_of_slot(i):
    return (i % 8) * 16 + ((i // 8) % 4) * 4 + ((i // 32) % 2) * 2 + i // 64


def forward_kernel(
    first, middle, window, last_t, last_tiles, gain, observed,
    theta, theta_last, mix_t,
    wf, mc, xw, h1, acc, part, part_in, every, hi_part, lo_part, gram, gram_in,
    y_send, y_recv, a_send, a_recv, l_send, l_recv, p_send, p_recv, s_send, s_recv, g_send, g_recv,
):
    me, y = lax.axis_index("member"), lax.axis_index("dp")
    barrier = pltpu.get_barrier_semaphore()
    for d in range(1, ND):
        pl.semaphore_signal(barrier, inc=1, device_id=(me, (y + d) % ND), device_id_type=MESH)

    def greet(i, carry):
        pl.semaphore_signal(barrier, inc=1, device_id=((me + i) % NM, y), device_id_type=MESH)
        return carry

    lax.fori_loop(1, NM, greet, 0)
    pl.semaphore_wait(barrier, NM - 1 + ND - 1)

    def y_copies(d):
        t = (y - d) % ND
        cols = pl.ds(pl.multiple_of(t * 512, 512), 512)
        jobs = ((window, xw.at[d]), (first, wf.at[d]), (middle.at[:, :, cols], mc.at[d]))
        out = []
        for k, (src, dst) in enumerate(jobs):
            if d == 0:
                out.append(pltpu.make_async_copy(src, dst, y_recv.at[k, d]))
            else:
                out.append(
                    pltpu.make_async_remote_copy(
                        src_ref=src, dst_ref=dst, send_sem=y_send.at[k, d], recv_sem=y_recv.at[k, d],
                        device_id=(me, t), device_id_type=MESH,
                    )
                )
        return out

    ys = [y_copies(d) for d in range(ND)]
    for k in range(3):
        for d in (0, 2, 1, 3):
            ys[d][k].start()

    def exchange(p, remote):
        mr, mcol = middle_block(p)
        fr, fcol = first_block(p)
        jobs = (
            (middle.at[:, mr, mcol], theta.at[pair(me), :, pl.ds(0, WIDE)]),
            (first.at[:, fr, fcol], theta.at[pair(me), :, pl.ds(WIDE, SLIM)]),
        )
        for src, dst in jobs:
            if remote:
                pltpu.make_async_remote_copy(
                    src_ref=src, dst_ref=dst, send_sem=a_send, recv_sem=a_recv, device_id=(p, y), device_id_type=MESH
                ).start()
            else:
                pltpu.make_async_copy(src, dst, a_recv).start()

    exchange(me, False)

    def send_one(step, carry):
        exchange(plane_peer(me, step), True)
        return carry

    lax.fori_loop(1, NM, send_one, 0)
    for t, owner in enumerate(LAST_OWNERS):
        @pl.when(me == owner)
        def _():
            pltpu.make_async_copy(last_tiles.at[:, t], theta_last.at[pair(me)], l_recv).start()

        @pl.when(me != owner)
        def _():
            pltpu.make_async_remote_copy(
                src_ref=last_tiles.at[:, t], dst_ref=theta_last.at[pair(me)], send_sem=l_send.at[t], recv_sem=l_recv,
                device_id=(owner, y), device_id_type=MESH,
            ).start()

    in_scale = F_IN ** (-0.5)
    hid_scale = H ** (-0.5)
    order = (0, 1, 3, 2)
    for k in (0, 1):
        for d in order:
            if d == 0:
                ys[d][k].wait()
            else:
                ys[d][k].wait_recv()

    for d in order:
        for m in range(2):
            def rows_one(i, carry, d=d, m=m):
                rows = pl.ds(pl.multiple_of(i * 256, 256), 256)
                z = jnp.dot(xw[i], wf[d, m], preferred_element_type=jnp.float32)
                h1[m, d, rows, :] = jnp.tanh(z * in_scale).astype(jnp.bfloat16)
                return carry

            lax.fori_loop(0, 4, rows_one, 0)
    for n, d in enumerate(order):
        if d == 0:
            ys[d][2].wait()
        else:
            ys[d][2].wait_recv()
        for m in range(2):
            def rows_two(i, carry, d=d, m=m, n=n):
                rows = pl.ds(pl.multiple_of(i * 256, 256), 256)
                z = jnp.dot(h1[m, d, rows, :], mc[d, m], preferred_element_type=jnp.float32)
                if n == 0:
                    acc[m, rows, :] = z
                elif n < ND - 1:
                    acc[m, rows, :] += z
                else:
                    h2 = jnp.tanh((acc[m, rows, :] + z) * hid_scale).astype(jnp.bfloat16)
                    here = lax.dot_general(
                        last_t[m], h2, (((1,), (1,)), ((), ())), preferred_element_type=jnp.float32
                    )
                    if m == 0:
                        part[i] = here
                    else:
                        part[i] += here
                return carry

            lax.fori_loop(0, 4, rows_two, 0)

    def part_copy(d):
        t = (y - d) % ND
        return pltpu.make_async_remote_copy(
            src_ref=part.at[(ND - d) % ND], dst_ref=part_in.at[d], send_sem=p_send.at[d], recv_sem=p_recv.at[d],
            device_id=(me, t), device_id_type=MESH,
        )

    ps = [part_copy(d) for d in range(1, ND)]
    for c in ps:
        c.start()
    for c in ps:
        c.wait_recv()
    total = part[0] + part_in[1] + part_in[2] + part_in[3]
    z, x, core = me // 8, (me // 2) % 4, me % 2

    every[core * 32 + x * 8 + z] = (total * hid_scale) * gain[:, 0:1]

    def spread(phase, first_slot, count, p):
        slots = every.at[pl.ds(first_slot, count)]
        return pltpu.make_async_remote_copy(
            src_ref=slots, dst_ref=slots, send_sem=s_send.at[phase], recv_sem=s_recv.at[phase],
            device_id=(p, y), device_id_type=MESH,
        )

    def whole_wait(sem, count):
        slots = every.at[pl.ds(0, count)]
        pltpu.make_async_copy(slots, slots, sem).wait()

    for i in range(1, 8):
        spread(0, core * 32 + x * 8 + z, 1, ((z + i) % 8) * 8 + x * 2 + core).start()
    whole_wait(s_recv.at[0], 7)
    for i in (2, 1, 3):
        spread(1, core * 32 + x * 8, 8, z * 8 + ((x + i) % 4) * 2 + core).start()
    whole_wait(s_recv.at[1], 24)
    spread(2, core * 32, 32, z * 8 + x * 2 + 1 - core).start()
    whole_wait(s_recv.at[2], 32)

    pull = jnp.zeros((ENS, 256), jnp.float32)
    for c in range(10):
        values = jnp.concatenate([every[:, c, :], every[:, 10 + c, :]], axis=0)
        center = jnp.mean(values, axis=0, keepdims=True)
        anomaly = values - center
        upper = anomaly.astype(jnp.bfloat16)
        hi_part[:, c * 256:(c + 1) * 256] = upper
        lo_part[:, c * 256:(c + 1) * 256] = (anomaly - upper.astype(jnp.float32)).astype(jnp.bfloat16)
        pull = pull + anomaly * (observed[c:c + 1, :] - center)
    over_samples = (((1,), (1,)), ((), ()))
    squares = lax.dot_general(hi_part[...], hi_part[...], over_samples, preferred_element_type=jnp.float32)
    crossed = lax.dot_general(hi_part[...], lo_part[...], over_samples, preferred_element_type=jnp.float32)
    gram[:ENS, :] = squares + (crossed + crossed.T)
    drive_tall = jnp.broadcast_to(jnp.sum(pull, axis=1, keepdims=True), (ENS, ENS))
    gram[ENS:, :] = drive_tall.T[:8, :]

    def gram_copy(d):
        return pltpu.make_async_remote_copy(
            src_ref=gram, dst_ref=gram_in.at[d - 1], send_sem=g_send.at[d], recv_sem=g_recv.at[d],
            device_id=(me, (y - d) % ND), device_id_type=MESH,
        )

    gs = [gram_copy(d) for d in range(1, ND)]
    for c in gs:
        c.start()
    for c in gs:
        c.wait_recv()
    summed = gram[...] + gram_in[0] + gram_in[1] + gram_in[2]
    diagonal = lax.broadcasted_iota(jnp.int32, (ENS, ENS), 0) == lax.broadcasted_iota(jnp.int32, (ENS, ENS), 1)
    inverse = spd_inverse(summed[:ENS] + jnp.where(diagonal, float(ENS), 0.0))
    lift = jnp.sum(inverse * summed[ENS:ENS + 1], axis=1, keepdims=True)
    mix_t[...] = (
        float(ENS) * (inverse - jnp.mean(inverse, axis=0, keepdims=True))
        + (lift - jnp.mean(lift, axis=0, keepdims=True))
        + 1.0 / ENS
    )

    for c in ps + gs:
        c.wait_send()
    whole_wait(s_send.at[0], 7)
    whole_wait(s_send.at[1], 24)
    whole_wait(s_send.at[2], 32)
    for d in range(1, ND):
        for c in ys[d]:
            c.wait_send()
    pltpu.make_async_copy(theta, theta, a_recv).wait()
    rest = theta.at[pl.ds(0, ENS - 2)]
    pltpu.make_async_copy(rest, rest, a_send).wait()
    for t, owner in enumerate(LAST_OWNERS):
        @pl.when(me == owner)
        def _():
            pltpu.make_async_copy(theta_last, theta_last, l_recv).wait()

        @pl.when(me != owner)
        def _():
            pltpu.make_async_copy(last_tiles.at[:, t], last_tiles.at[:, t], l_send.at[t]).wait()


def update_kernel(
    theta_hbm, theta_last_hbm, mix_t,
    new_first, new_middle, new_last,
    theta, theta_last, wide_hi, wide_lo, out, out_last,
    in_sem, a_send, m_recv, f_recv, l_send, l_recv,
):
    me, y = lax.axis_index("member"), lax.axis_index("dp")
    barrier = pltpu.get_barrier_semaphore()

    def greet(i, carry):
        pl.semaphore_signal(barrier, inc=1, device_id=((me + i) % NM, y), device_id_type=MESH)
        return carry

    lax.fori_loop(1, NM, greet, 0)
    is_owner = (me == LAST_OWNERS[0]) | (me == LAST_OWNERS[1]) | (me == LAST_OWNERS[2])
    load = pltpu.make_async_copy(theta_hbm, theta, in_sem.at[0])
    load.start()
    load_last = pltpu.make_async_copy(theta_last_hbm, theta_last, in_sem.at[1])
    load_last.start()

    hi = mix_t[...].astype(jnp.bfloat16)
    lo = (mix_t[...] - hi.astype(jnp.float32)).astype(jnp.bfloat16)
    size = ENS * TILE
    spread_t = (
        member_of_slot(lax.broadcasted_iota(jnp.int32, (ENS, size), 0))
        == lax.broadcasted_iota(jnp.int32, (ENS, size), 1) // TILE
    ).astype(jnp.bfloat16)
    block = 256

    def widen(i, carry):
        rows = pl.ds(pl.multiple_of(i * block, block), block)
        row_id = lax.broadcasted_iota(jnp.int32, (block, ENS), 0) + i * block
        spread = (row_id // TILE == member_of_slot(lax.broadcasted_iota(jnp.int32, (block, ENS), 1))).astype(jnp.bfloat16)
        keep = (
            lax.broadcasted_iota(jnp.int32, (block, size), 0) % TILE
            == lax.broadcasted_iota(jnp.int32, (block, size), 1) % TILE
        )
        for source, target in ((hi, wide_hi), (lo, wide_lo)):
            tall = lax.dot_general(
                spread, source, (((1,), (1,)), ((), ())), preferred_element_type=jnp.float32
            ).astype(jnp.bfloat16)
            full = jnp.dot(tall, spread_t, preferred_element_type=jnp.float32)
            target[rows, :] = jnp.where(keep, full, 0.0).astype(jnp.bfloat16)
        return carry

    lax.fori_loop(0, size // block, widen, 0)
    load.wait()
    load_last.wait()
    pl.semaphore_wait(barrier, NM - 1)

    mr, mcol = middle_block(me)
    fr, fcol = first_block(me)

    def results(p, remote):
        jobs = (
            (out.at[pair(p), :, pl.ds(0, WIDE)], new_middle.at[:, mr, mcol], m_recv),
            (out.at[pair(p), :, pl.ds(WIDE, SLIM)], new_first.at[:, fr, fcol], f_recv),
        )
        for src, dst, sem in jobs:
            if remote:
                pltpu.make_async_remote_copy(
                    src_ref=src, dst_ref=dst, send_sem=a_send, recv_sem=sem, device_id=(p, y), device_id_type=MESH
                ).start()
            else:
                pltpu.make_async_copy(src, dst, sem).start()

    def one_plane(b, carry):
        plane = (me // 8 + b) % 8
        rows = pl.ds(pl.multiple_of(plane * block, block), block)
        members = pl.ds(pl.multiple_of(plane * 16, 16), 16)
        flat = theta[...].reshape(size, WIDE + SLIM)
        z = jnp.dot(wide_hi[rows, :], flat, preferred_element_type=jnp.float32)
        z += jnp.dot(wide_lo[rows, :], flat, preferred_element_type=jnp.float32)
        out[members] = z.astype(jnp.bfloat16).reshape(16, TILE, WIDE + SLIM)

        def send_one(c, inner):
            p = plane * 8 + (me % 8 + c) % 8

            @pl.when(p != me)
            def _():
                results(p, True)

            @pl.when(p == me)
            def _():
                results(p, False)

            return inner

        lax.fori_loop(0, 8, send_one, 0)
        return carry

    lax.fori_loop(0, 8, one_plane, 0)

    @pl.when(is_owner)
    def _():
        flat = theta_last[...].reshape(size, SLIM)

        def one(i, carry):
            rows = pl.ds(pl.multiple_of(i * block, block), block)
            z = jnp.dot(wide_hi[rows, :], flat, preferred_element_type=jnp.float32)
            z += jnp.dot(wide_lo[rows, :], flat, preferred_element_type=jnp.float32)
            out_last[pl.ds(pl.multiple_of(i * 16, 16), 16)] = z.astype(jnp.bfloat16).reshape(16, TILE, SLIM)
            return carry

        lax.fori_loop(0, 8, one, 0)

    for t, owner in enumerate(LAST_OWNERS):
        @pl.when(me == owner)
        def _():
            pltpu.make_async_copy(out_last.at[pair(me)], new_last.at[:, t], l_recv).start()

            def send_last(i, carry):
                p = (me + i) % NM
                pltpu.make_async_remote_copy(
                    src_ref=out_last.at[pair(p)], dst_ref=new_last.at[:, t], send_sem=l_send, recv_sem=l_recv,
                    device_id=(p, y), device_id_type=MESH,
                ).start()
                return carry

            lax.fori_loop(1, NM, send_last, 0)
            sent = out_last.at[pl.ds(0, ENS - 2)]
            pltpu.make_async_copy(sent, sent, l_send).wait()

    pltpu.make_async_copy(new_middle, new_middle, m_recv).wait()
    pltpu.make_async_copy(new_first, new_first, f_recv).wait()
    pltpu.make_async_copy(new_last, new_last, l_recv).wait()
    rest = out.at[pl.ds(0, ENS - 2)]
    pltpu.make_async_copy(rest, rest, a_send).wait()


def on_device(
    feature_pool, labels, sample_rows, noise_variance, first_weight, middle_weight, last_weight
):
    local_count = sample_rows.shape[0]
    members_here = first_weight.shape[0]
    classes_total = noise_variance.shape[0]
    window = feature_pool[sample_rows]
    classes = labels[sample_rows]
    target = (classes[None, :] == jnp.arange(16, dtype=jnp.int32)[:, None]).astype(jnp.float32)
    whiten = 1.0 / jnp.sqrt(noise_variance)
    observed = target * jnp.pad(whiten, (0, 16 - classes_total))[:, None]
    gain = jnp.broadcast_to(jnp.pad(jnp.tile(whiten, 2), (0, ROWS - 2 * classes_total))[:, None], (ROWS, 128))
    turned = jnp.swapaxes(last_weight, 1, 2)
    last_t = jnp.stack([
        jnp.pad(turned[m], ((m * classes_total, ROWS - (m + 1) * classes_total), (0, 0))) for m in range(members_here)
    ])
    per_member = last_weight.shape[1] * classes_total
    padded = LAST_TILES * TILE * SLIM
    last_tiles = jnp.pad(last_weight.reshape(members_here, per_member), ((0, 0), (0, padded - per_member)))
    last_tiles = last_tiles.reshape(members_here, LAST_TILES, TILE, SLIM)

    anyspace = pl.BlockSpec(memory_space=pl.ANY)
    vmem = pl.BlockSpec(memory_space=pltpu.VMEM)
    bf16, f32 = jnp.bfloat16, jnp.float32
    theta, theta_last, mix_t = pl.pallas_call(
        forward_kernel,
        out_shape=(
            jax.ShapeDtypeStruct((ENS, TILE, WIDE + SLIM), bf16),
            jax.ShapeDtypeStruct((ENS, TILE, SLIM), bf16),
            jax.ShapeDtypeStruct((ENS, ENS), f32),
        ),
        in_specs=[anyspace, anyspace, anyspace, vmem, anyspace, vmem, vmem],
        out_specs=(anyspace, anyspace, vmem),
        scratch_shapes=[
            pltpu.VMEM((ND, 2, 256, 512), bf16),
            pltpu.VMEM((ND, 2, 512, 512), bf16),
            pltpu.VMEM((ND, 256, 256), bf16),
            pltpu.VMEM((2, ND, 1024, 512), bf16),
            pltpu.VMEM((2, 1024, 512), f32),
            pltpu.VMEM((ND, ROWS, 256), f32),
            pltpu.VMEM((ND, ROWS, 256), f32),
            pltpu.VMEM((NM, ROWS, 256), f32),
            pltpu.VMEM((ENS, 2560), bf16),
            pltpu.VMEM((ENS, 2560), bf16),
            pltpu.VMEM((ENS + 8, ENS), f32),
            pltpu.VMEM((ND - 1, ENS + 8, ENS), f32),
            pltpu.SemaphoreType.DMA((3, ND)),
            pltpu.SemaphoreType.DMA((3, ND)),
            pltpu.SemaphoreType.DMA,
            pltpu.SemaphoreType.DMA,
            pltpu.SemaphoreType.DMA((LAST_TILES,)),
            pltpu.SemaphoreType.DMA,
            pltpu.SemaphoreType.DMA((ND,)),
            pltpu.SemaphoreType.DMA((ND,)),
            pltpu.SemaphoreType.DMA((3,)),
            pltpu.SemaphoreType.DMA((3,)),
            pltpu.SemaphoreType.DMA((ND,)),
            pltpu.SemaphoreType.DMA((ND,)),
        ],
        compiler_params=pltpu.CompilerParams(collective_id=0, has_side_effects=True, vmem_limit_bytes=VMEM_LIMIT),
    )(first_weight, middle_weight, window, last_t, last_tiles, gain, observed)

    new_first, new_middle, new_last = pl.pallas_call(
        update_kernel,
        out_shape=(
            jax.ShapeDtypeStruct(first_weight.shape, bf16),
            jax.ShapeDtypeStruct(middle_weight.shape, bf16),
            jax.ShapeDtypeStruct(last_tiles.shape, bf16),
        ),
        in_specs=[anyspace, anyspace, vmem],
        out_specs=(anyspace, anyspace, anyspace),
        scratch_shapes=[
            pltpu.VMEM((ENS, TILE, WIDE + SLIM), bf16),
            pltpu.VMEM((ENS, TILE, SLIM), bf16),
            pltpu.VMEM((ENS * TILE, ENS * TILE), bf16),
            pltpu.VMEM((ENS * TILE, ENS * TILE), bf16),
            pltpu.VMEM((ENS, TILE, WIDE + SLIM), bf16),
            pltpu.VMEM((ENS, TILE, SLIM), bf16),
            pltpu.SemaphoreType.DMA((2,)),
            pltpu.SemaphoreType.DMA,
            pltpu.SemaphoreType.DMA,
            pltpu.SemaphoreType.DMA,
            pltpu.SemaphoreType.DMA,
            pltpu.SemaphoreType.DMA,
        ],
        compiler_params=pltpu.CompilerParams(collective_id=1, has_side_effects=True, vmem_limit_bytes=VMEM_LIMIT),
    )(theta, theta_last, mix_t)
    new_last = new_last.reshape(members_here, padded)[:, :per_member].reshape(last_weight.shape)
    return (new_first, new_middle, new_last)


def solution(mesh):
    in_specs = (
        P("dp", None),
        P("dp"),
        P("dp"),
        P(),
        P("member", None, "dp"),
        P("member", "dp", None),
        P("member", "dp", None),
    )
    out_specs = (P("member", None, "dp"), P("member", "dp", None), P("member", "dp", None))
    return jax.shard_map(
        on_device, mesh=mesh, in_specs=in_specs, out_specs=out_specs, check_vma=False
    )
```

```python
import functools

import jax
import jax.numpy as jnp
from jax import lax
from jax.experimental import pallas as pl
from jax.experimental.pallas import tpu as pltpu
from jax.sharding import PartitionSpec as P

F_IN = 256
H = 2048
MESH = pl.DeviceIdType.MESH
NM = 64
ND = 4
ENS = 128
CLASSES = 10
TILE = 16
WIDE = 1024
SLIM = 128
VMEM_LIMIT = 60 * 1024 * 1024
OVER_LAST = (((1,), (1,)), ((), ()))
OVER_FIRST = (((0,), (0,)), ((), ()))


def dot32(a, b, dims=(((1,), (0,)), ((), ()))):
    return lax.dot_general(a, b, dims, preferred_element_type=jnp.float32)


def iota(shape, dim):
    return lax.broadcasted_iota(jnp.int32, shape, dim)


def middle_block(p):
    return pl.ds(pl.multiple_of((p // 2) * TILE, TILE), TILE), pl.ds(pl.multiple_of((p % 2) * WIDE, WIDE), WIDE)


def first_block(p):
    return pl.ds(pl.multiple_of((p // 4) * TILE, TILE), TILE), pl.ds(pl.multiple_of((p % 4) * SLIM, SLIM), SLIM)


def pair(p):
    return pl.ds(pl.multiple_of(2 * p, 2), 2)


def swing(turn):
    up = (turn + 1) // 2
    out = (turn % 2) * up + (1 - turn % 2) * (8 - up)
    far = (7 - turn) // 7
    return (out * (1 - far) + 4 * far - 4 * (turn // 7)) % 8


def whole_wait(ref, sem):
    pltpu.make_async_copy(ref, ref, sem).wait()


def spd_inverse(system):
    size = system.shape[0]
    group = 8
    sub = iota((group, size), 0)
    lane = iota((group, size), 1)
    lanes = iota((size - group, size), 1)

    def one_round(_, a):
        panel = a[:group, :]
        for k in range(group):
            row = panel[k:k + 1, :]
            col = panel[:, k:k + 1]
            pivot = 1.0 / row[:, k:k + 1]
            row = jnp.where(lane[:1] == k, pivot, row * pivot)
            panel = jnp.where(sub == k, row, jnp.where(lane == k, 0.0, panel) - col * row)
        below = jnp.where(lanes < group, 0.0, a[group:, :])
        for k in range(group):
            below = below - a[group:, k:k + 1] * panel[k:k + 1, :]
        turned = jnp.concatenate([below, panel], axis=0)
        return pltpu.roll(turned, size - group, 1)

    return lax.fori_loop(0, size // group, one_round, system)


def member_of_slot(i):
    return (i % 8) * 16 + ((i // 8) % 4) * 4 + i // 32


def kernel(
    first, middle, pool, labels, rows_picked, last, variance,
    new_first, new_middle, new_last,
    theta, theta_last, wf, mc, xw, h1, acc, lt, last_rows, part, part_in, every, hi_part, lo_part, gram, gram_in,
    mix_hi, mix_lo, wide_hi, wide_lo, out, out_last,
    x_send, x_recv, f_send, f_recv, m_send, m_recv, t_send, t_recv,
    a_send, a_recv, l_send, l_recv, p_send, p_recv, s_send, s_recv, g_send, g_recv,
    u_send, um_recv, uf_recv, ul_send, ul_recv,
):
    bf16, f32 = jnp.bfloat16, jnp.float32
    me, y = lax.axis_index("member"), lax.axis_index("dp")
    z, x, core = me // 8, (me // 2) % 4, me % 2
    chip = me - core
    barrier = pltpu.get_barrier_semaphore()
    for c in range(2):
        for d in range(1, ND):
            pl.semaphore_signal(barrier, inc=1, device_id=(chip + c, (y + d) % ND), device_id_type=MESH)

    def greet(i, carry):
        pl.semaphore_signal(barrier, inc=1, device_id=((me + i) % NM, y), device_id_type=MESH)
        return carry

    lax.fori_loop(1, NM, greet, 0)

    picked = (iota((512, 256), 0) == rows_picked[...]).astype(bf16)
    xw[0] = dot32(picked, pool[...], OVER_FIRST).astype(bf16)
    target = dot32((iota((16, 512), 0) == labels[...]).astype(bf16), picked)
    turn_classes = (iota((16, CLASSES), 0) == iota((16, CLASSES), 1)).astype(bf16)
    for m in range(2):
        last_rows[m] = dot32(turn_classes, last[m], OVER_LAST).astype(bf16)
    spread_var = jnp.ones((16, 128), f32)
    for c in range(CLASSES):
        spread_var = jnp.where(iota((16, 128), 0) == c, variance[c], spread_var)
    gain = 1.0 / jnp.sqrt(spread_var)
    observed = jnp.where(core == 0, target[:, :128], target[:, 128:]) * gain

    pl.semaphore_wait(barrier, NM - 1 + 2 * (ND - 1))

    def x_copy(d):
        return pltpu.make_async_remote_copy(
            src_ref=xw.at[0], dst_ref=xw.at[d], send_sem=x_send.at[d], recv_sem=x_recv.at[d],
            device_id=(me, (y - d) % ND), device_id_type=MESH,
        )

    def give(src, dst, send_sem, recv_sem, c, t, waiting=False):
        away = (t != y) | (c != core)

        @pl.when(away)
        def _():
            copy = pltpu.make_async_remote_copy(
                src_ref=src, dst_ref=dst, send_sem=send_sem, recv_sem=recv_sem, device_id=(chip + c, t), device_id_type=MESH
            )
            if waiting:
                copy.wait_send()
            else:
                copy.start()

        if not waiting:
            @pl.when(jnp.logical_not(away))
            def _():
                pltpu.make_async_copy(src, dst, recv_sem).start()

    def give_first(waiting):
        for m in range(2):
            t = 2 * core + m
            slot = (y - t) % ND
            for c in range(2):
                give(first.at[m], wf.at[slot], f_send.at[m, c], f_recv.at[slot], c, t, waiting)
            give(last_rows.at[m], lt.at[y % 2], t_send.at[m], t_recv.at[y % 2], y // 2, t, waiting)

    def give_middle(waiting):
        for half in range(2):
            for m in range(2):
                t = 2 * core + m
                slot = (y - t) % ND
                for c in range(2):
                    src = middle.at[m, :, pl.ds(c * 1024 + half * 512, 512)]
                    give(src, mc.at[half, slot], m_send.at[half, m, c], m_recv.at[half, slot], c, t, waiting)

    for d in (2, 1, 3):
        x_copy(d).start()
    give_first(False)
    give_middle(False)

    def exchange(p, remote):
        mr, mcol = middle_block(p)
        fr, fcol = first_block(p)
        jobs = (
            (middle.at[:, mr, mcol], theta.at[pair(me), :, pl.ds(0, WIDE)]),
            (first.at[:, fr, fcol], theta.at[pair(me), :, pl.ds(WIDE, SLIM)]),
        )
        for src, dst in jobs:
            if remote:
                pltpu.make_async_remote_copy(
                    src_ref=src, dst_ref=dst, send_sem=a_send, recv_sem=a_recv, device_id=(p, y), device_id_type=MESH
                ).start()
            else:
                pltpu.make_async_copy(src, dst, a_recv).start()

    def send_one(step, carry):
        p = ((z + swing(step % 8)) % 8) * 8 + (me % 8 + step // 8) % 8

        @pl.when(p != me)
        def _():
            exchange(p, True)

        @pl.when(p == me)
        def _():
            exchange(p, False)

        return carry

    lax.fori_loop(0, NM, send_one, 0)
    for t in range(4):
        owner = 3 + 17 * t
        src = last_rows.at[:, :, pl.ds(t * 128, 128)]

        @pl.when(me == owner)
        def _():
            pltpu.make_async_copy(src, theta_last.at[pair(me)], l_recv).start()

        @pl.when(me != owner)
        def _():
            pltpu.make_async_remote_copy(
                src_ref=src, dst_ref=theta_last.at[pair(me)], send_sem=l_send.at[t], recv_sem=l_recv,
                device_id=(owner, y), device_id_type=MESH,
            ).start()

    in_scale = F_IN ** (-0.5)
    hid_scale = H ** (-0.5)
    order = (0, 1, 3, 2)
    for d in (1, 3, 2):
        x_copy(d).wait_recv()
    for d in order:
        whole_wait(wf.at[d], f_recv.at[d])

        def rows_one(i, carry, d=d):
            rows = pl.ds(pl.multiple_of(i * 256, 256), 256)
            h1[d, rows, :] = jnp.tanh(dot32(xw[i], wf[d]) * in_scale).astype(bf16)
            return carry

        lax.fori_loop(0, 4, rows_one, 0)
    for s in range(2):
        whole_wait(lt.at[s], t_recv.at[s])
    for half in range(2):
        for n, d in enumerate(order):
            whole_wait(mc.at[half, d], m_recv.at[half, d])

            def rows_two(i, carry, d=d, n=n, half=half):
                rows = pl.ds(pl.multiple_of(i * 256, 256), 256)
                term = dot32(h1[d, rows, :], mc[half, d])
                if n == 0:
                    acc[rows, :] = term
                elif n < ND - 1:
                    acc[rows, :] += term
                else:
                    h2 = jnp.tanh((acc[rows, :] + term) * hid_scale).astype(bf16)
                    here = dot32(lt[half], h2, OVER_LAST)
                    for c in range(2):
                        piece = here[:, c * 128:(c + 1) * 128]
                        if half == 0:
                            part[i, c] = piece
                        else:
                            part[i, c] += piece
                return carry

            lax.fori_loop(0, 4, rows_two, 0)

    mine = core * ND + y
    def part_copy(d, c):
        return pltpu.make_async_remote_copy(
            src_ref=part.at[d, c], dst_ref=part_in.at[mine], send_sem=p_send, recv_sem=p_recv,
            device_id=(chip + c, (y + d) % ND), device_id_type=MESH,
        )

    for c in range(2):
        for d in range(ND):
            if d == 0:
                @pl.when(core != c)
                def _():
                    part_copy(0, c).start()

                @pl.when(core == c)
                def _():
                    part_in[mine] = part[0, c]
            else:
                part_copy(d, c).start()
    whole_wait(part_in.at[pl.ds(0, 7)], p_recv)
    scaled = [((part_in[s] + part_in[ND + s]) * hid_scale * gain)[:CLASSES] for s in range(ND)]
    every[x * 8 + z] = jnp.concatenate(scaled, axis=0)

    def spread(phase, first_slot, count, p):
        slots = every.at[pl.ds(first_slot, count)]
        return pltpu.make_async_remote_copy(
            src_ref=slots, dst_ref=slots, send_sem=s_send.at[phase], recv_sem=s_recv.at[phase],
            device_id=(p, y), device_id_type=MESH,
        )

    for i in (4, 3, 5, 2, 6, 1, 7):
        spread(0, x * 8 + z, 1, ((z + i) % 8) * 8 + x * 2 + core).start()
    whole_wait(every.at[pl.ds(0, 7)], s_recv.at[0])
    for i in (2, 1, 3):
        spread(1, pl.multiple_of(x * 8, 8), 8, z * 8 + ((x + i) % 4) * 2 + core).start()
    whole_wait(every.at[pl.ds(0, 24)], s_recv.at[1])

    pull = jnp.zeros((ENS, 128), f32)
    for c in range(CLASSES):
        values = jnp.concatenate([every[:, s * CLASSES + c, :] for s in range(ND)], axis=0)
        center = jnp.mean(values, axis=0, keepdims=True)
        anomaly = values - center
        upper = anomaly.astype(bf16)
        hi_part[:, c * 128:(c + 1) * 128] = upper
        lo_part[:, c * 128:(c + 1) * 128] = (anomaly - upper.astype(f32)).astype(bf16)
        pull = pull + anomaly * (observed[c:c + 1, :] - center)
    squares = dot32(hi_part[...], hi_part[...], OVER_LAST)
    crossed = dot32(hi_part[...], lo_part[...], OVER_LAST)
    gram[:ENS, :] = squares + (crossed + crossed.T)
    drive_tall = jnp.broadcast_to(jnp.sum(pull, axis=1, keepdims=True), (ENS, ENS))
    gram[ENS:, :] = drive_tall.T[:8, :]

    def gram_copy(k):
        dc, dy = k // ND, k % ND
        return pltpu.make_async_remote_copy(
            src_ref=gram, dst_ref=gram_in.at[k - 1], send_sem=g_send, recv_sem=g_recv,
            device_id=(chip + (core + dc) % 2, (y + dy) % ND), device_id_type=MESH,
        )

    for k in (2, 6, 1, 3, 5, 7, 4):
        gram_copy(k).start()
    whole_wait(gram_in, g_recv)
    summed = gram[...]
    for k in range(7):
        summed = summed + gram_in[k]
    diagonal = iota((ENS, ENS), 0) == iota((ENS, ENS), 1)
    inverse = spd_inverse(summed[:ENS] + jnp.where(diagonal, float(ENS), 0.0))
    lift = jnp.sum(inverse * summed[ENS:ENS + 1], axis=1, keepdims=True)
    mix_t = (
        float(ENS) * (inverse - jnp.mean(inverse, axis=0, keepdims=True))
        + (lift - jnp.mean(lift, axis=0, keepdims=True))
        + 1.0 / ENS
    )
    upper = mix_t.astype(bf16)
    size = ENS * TILE
    natural = (iota((ENS, ENS), 0) == member_of_slot(iota((ENS, ENS), 1))).astype(bf16)
    mix_hi[...] = dot32(natural, upper).astype(bf16)
    mix_lo[...] = dot32(natural, (mix_t - upper.astype(f32)).astype(bf16)).astype(bf16)

    whole_wait(theta, a_recv)
    is_owner = (me - 3) % 17 == 0
    my_tile = pl.ds(pl.multiple_of(((me + 14) // 17 - 1) % 4 * 128, 128), 128)

    @pl.when(is_owner)
    def _():
        whole_wait(theta_last, l_recv)

    mr, mcol = middle_block(me)
    fr, fcol = first_block(me)

    def results(slot, p, remote):
        jobs = (
            (out.at[pair(slot), :, pl.ds(0, WIDE)], new_middle.at[:, mr, mcol], um_recv),
            (out.at[pair(slot), :, pl.ds(WIDE, SLIM)], new_first.at[:, fr, fcol], uf_recv),
        )
        for src, dst, sem in jobs:
            if remote:
                pltpu.make_async_remote_copy(
                    src_ref=src, dst_ref=dst, send_sem=u_send, recv_sem=sem, device_id=(p, y), device_id_type=MESH
                ).start()
            else:
                pltpu.make_async_copy(src, dst, sem).start()

        @pl.when(is_owner)
        def _():
            src, dst = out_last.at[pair(slot)], new_last.at[:, :, my_tile]
            if remote:
                pltpu.make_async_remote_copy(
                    src_ref=src, dst_ref=dst, send_sem=ul_send, recv_sem=ul_recv, device_id=(p, y), device_id_type=MESH
                ).start()
            else:
                pltpu.make_async_copy(src, dst, ul_recv).start()

    block = 256

    def one_block(b, carry):
        low = (me % 8 + b) % 8
        k = iota((block, ENS), 0) // TILE
        member = ((k // 2) * 8 + low) * 2 + k % 2
        choose = (member == member_of_slot(iota((block, ENS), 1))).astype(bf16)
        repeat = (iota((ENS, size), 0) == iota((ENS, size), 1) // TILE).astype(bf16)
        keep = (iota((block, size), 0) % TILE) == (iota((block, size), 1) % TILE)
        for source, wide in ((mix_hi, wide_hi), (mix_lo, wide_lo)):
            tall = dot32(choose, source[...], OVER_LAST).astype(bf16)
            wide[...] = jnp.where(keep, dot32(tall, repeat), 0.0).astype(bf16)
        flat = theta[...].reshape(size, WIDE + SLIM)
        mixed = dot32(wide_hi[...], flat) + dot32(wide_lo[...], flat)
        here = pl.ds(pl.multiple_of(b * 16, 16), 16)
        out[here] = mixed.astype(bf16).reshape(16, TILE, WIDE + SLIM)

        @pl.when(is_owner)
        def _():
            tiles = theta_last[...].reshape(size, SLIM)
            done = dot32(wide_hi[...], tiles) + dot32(wide_lo[...], tiles)
            out_last[here] = done.astype(bf16).reshape(16, TILE, SLIM)

        def send_result(turn, inner):
            there = (z + swing(turn)) % 8
            p = there * 8 + low
            slot = b * 8 + there

            @pl.when(p != me)
            def _():
                results(slot, p, True)

            @pl.when(p == me)
            def _():
                results(slot, p, False)

            return inner

        lax.fori_loop(0, 8, send_result, 0)
        return carry

    lax.fori_loop(0, 8, one_block, 0)

    for d in range(1, ND):
        x_copy(d).wait_send()
    give_first(True)
    give_middle(True)
    rest = pl.ds(0, ENS - 2)
    whole_wait(theta.at[rest], a_send)
    for t in range(4):
        @pl.when(me != 3 + 17 * t)
        def _():
            whole_wait(last_rows.at[:, :, pl.ds(t * 128, 128)], l_send.at[t])
    whole_wait(part_in.at[pl.ds(0, 7)], p_send)
    whole_wait(every.at[pl.ds(0, 7)], s_send.at[0])
    whole_wait(every.at[pl.ds(0, 24)], s_send.at[1])
    whole_wait(gram_in, g_send)
    whole_wait(new_middle, um_recv)
    whole_wait(new_first, uf_recv)
    whole_wait(new_last, ul_recv)
    whole_wait(out.at[rest], u_send)

    @pl.when(is_owner)
    def _():
        whole_wait(out_last.at[rest], ul_send)


def on_device(
    feature_pool, labels, sample_rows, noise_variance, first_weight, middle_weight, last_weight
):
    anyspace = pl.BlockSpec(memory_space=pl.ANY)
    vmem = pl.BlockSpec(memory_space=pltpu.VMEM)
    smem = pl.BlockSpec(memory_space=pltpu.SMEM)
    bf16, f32 = jnp.bfloat16, jnp.float32
    dma = pltpu.SemaphoreType.DMA
    new_first, new_middle, new_last = pl.pallas_call(
        kernel,
        out_shape=(
            jax.ShapeDtypeStruct(first_weight.shape, bf16),
            jax.ShapeDtypeStruct(middle_weight.shape, bf16),
            jax.ShapeDtypeStruct((2, TILE, 512), bf16),
        ),
        in_specs=[anyspace, anyspace, vmem, vmem, vmem, vmem, smem],
        out_specs=(anyspace, anyspace, anyspace),
        scratch_shapes=[
            pltpu.VMEM((ENS, TILE, WIDE + SLIM), bf16),
            pltpu.VMEM((ENS, TILE, SLIM), bf16),
            pltpu.VMEM((ND, 256, 512), bf16),
            pltpu.VMEM((2, ND, 512, 512), bf16),
            pltpu.VMEM((ND, 256, 256), bf16),
            pltpu.VMEM((ND, 1024, 512), bf16),
            pltpu.VMEM((1024, 512), f32),
            pltpu.VMEM((2, TILE, 512), bf16),
            pltpu.VMEM((2, TILE, 512), bf16),
            pltpu.VMEM((ND, 2, 16, 128), f32),
            pltpu.VMEM((2 * ND, 16, 128), f32),
            pltpu.VMEM((32, ND * CLASSES, 128), f32),
            pltpu.VMEM((ENS, CLASSES * 128), bf16),
            pltpu.VMEM((ENS, CLASSES * 128), bf16),
            pltpu.VMEM((ENS + 8, ENS), f32),
            pltpu.VMEM((7, ENS + 8, ENS), f32),
            pltpu.VMEM((ENS, ENS), bf16),
            pltpu.VMEM((ENS, ENS), bf16),
            pltpu.VMEM((256, ENS * TILE), bf16),
            pltpu.VMEM((256, ENS * TILE), bf16),
            pltpu.VMEM((ENS, TILE, WIDE + SLIM), bf16),
            pltpu.VMEM((ENS, TILE, SLIM), bf16),
            dma((ND,)), dma((ND,)),
            dma((2, 2)), dma((ND,)),
            dma((2, 2, 2)), dma((2, ND)),
            dma((2,)), dma((2,)),
            dma, dma,
            dma((4,)), dma,
            dma, dma,
            dma((2,)), dma((2,)),
            dma, dma,
            dma, dma, dma, dma, dma,
        ],
        compiler_params=pltpu.CompilerParams(collective_id=0, has_side_effects=True, vmem_limit_bytes=VMEM_LIMIT),
    )(
        first_weight, middle_weight, feature_pool, labels.reshape(1, -1), sample_rows.reshape(1, -1), last_weight,
        noise_variance,
    )
    new_last = jnp.swapaxes(new_last[:, :CLASSES, :], 1, 2)
    return (new_first, new_middle, new_last)


def solution(mesh):
    in_specs = (
        P("dp", None),
        P("dp"),
        P("dp"),
        P(),
        P("member", None, "dp"),
        P("member", "dp", None),
        P("member", "dp", None),
    )
    out_specs = (P("member", None, "dp"), P("member", "dp", None), P("member", "dp", None))
    return jax.shard_map(
        on_device, mesh=mesh, in_specs=in_specs, out_specs=out_specs, check_vma=False
    )
```

```python
import functools

import jax
import jax.numpy as jnp
from jax import lax
from jax.experimental import pallas as pl
from jax.experimental.pallas import tpu as pltpu
from jax.sharding import PartitionSpec as P

F_IN = 256
H = 2048
MESH = pl.DeviceIdType.MESH
NM = 64
ND = 4
ENS = 128
CLASSES = 10
CUTS = (40, 40, 40, 56)
TILE = 16
WIDE = 1024
SLIM = 128
VMEM_LIMIT = 60 * 1024 * 1024
OVER_LAST = (((1,), (1,)), ((), ()))
OVER_FIRST = (((0,), (0,)), ((), ()))


def dot32(a, b, dims=(((1,), (0,)), ((), ()))):
    return lax.dot_general(a, b, dims, preferred_element_type=jnp.float32)


def iota(shape, dim):
    return lax.broadcasted_iota(jnp.int32, shape, dim)


def middle_block(p):
    return pl.ds(pl.multiple_of((p // 2) * TILE, TILE), TILE), pl.ds(pl.multiple_of((p % 2) * WIDE, WIDE), WIDE)


def first_block(p):
    return pl.ds(pl.multiple_of((p // 4) * TILE, TILE), TILE), pl.ds(pl.multiple_of((p % 4) * SLIM, SLIM), SLIM)


def pair(p):
    return pl.ds(pl.multiple_of(2 * p, 2), 2)


def swing(turn):
    up = (turn + 1) // 2
    out = (turn % 2) * up + (1 - turn % 2) * (8 - up)
    far = (7 - turn) // 7
    return (out * (1 - far) + 4 * far - 4 * (turn // 7)) % 8


def whole_wait(ref, sem):
    pltpu.make_async_copy(ref, ref, sem).wait()


def spd_inverse(system):
    size = system.shape[0]
    group = 8
    sub = iota((group, size), 0)
    lane = iota((group, size), 1)
    lanes = iota((size - group, size), 1)

    def one_round(_, a):
        panel = a[:group, :]
        for k in range(0, group, 2):
            one, two = panel[k:k + 1, :], panel[k + 1:k + 2, :]
            col_one, col_two = panel[:, k:k + 1], panel[:, k + 1:k + 2]
            at_one, at_two = lane == k, lane == k + 1
            p, q = one[:, k:k + 1], one[:, k + 1:k + 2]
            r, t = two[:, k:k + 1], two[:, k + 1:k + 2]
            scale = 1.0 / (p * t - q * r)
            one = jnp.where(at_one[:1], 1.0, jnp.where(at_two[:1], 0.0, one))
            two = jnp.where(at_one[:1], 0.0, jnp.where(at_two[:1], 1.0, two))
            one, two = (t * one - q * two) * scale, (p * two - r * one) * scale
            rest = jnp.where(at_one | at_two, 0.0, panel) - col_one * one - col_two * two
            panel = jnp.where(sub == k, one, jnp.where(sub == k + 1, two, rest))
        below = jnp.where(lanes < group, 0.0, a[group:, :])
        for k in range(group):
            below = below - a[group:, k:k + 1] * panel[k:k + 1, :]
        turned = jnp.concatenate([below, panel], axis=0)
        return pltpu.roll(turned, size - group, 1)

    return lax.fori_loop(0, size // group, one_round, system)


def member_of_slot(i):
    return (i % 8) * 16 + ((i // 8) % 4) * 4 + i // 32


def kernel(
    first, middle, pool, labels, rows_picked, last, variance,
    new_first, new_middle, new_last,
    theta, theta_last, wf, mc, xw, h1, acc, lt, last_rows, part, part_in, every, hi_part, lo_part, gram, gram_in,
    mix_hi, mix_lo, wide_hi, wide_lo, out, out_last,
    x_send, x_recv, f_send, f_recv, m_send, m_recv, t_send, t_recv,
    a_send, a_recv, l_send, l_recv, p_send, p_recv, s_send, s_recv, g_send, g_recv,
    u_send, um_recv, uf_recv, ul_send, ul_recv,
):
    bf16, f32 = jnp.bfloat16, jnp.float32
    me, y = lax.axis_index("member"), lax.axis_index("dp")
    z, x, core = me // 8, (me // 2) % 4, me % 2
    chip = me - core
    barrier = pltpu.get_barrier_semaphore()
    for c in range(2):
        for d in range(1, ND):
            pl.semaphore_signal(barrier, inc=1, device_id=(chip + c, (y + d) % ND), device_id_type=MESH)

    def greet(i, carry):
        pl.semaphore_signal(barrier, inc=1, device_id=((me + i) % NM, y), device_id_type=MESH)
        return carry

    lax.fori_loop(1, NM, greet, 0)

    picked = (iota((512, 256), 0) == rows_picked[...]).astype(bf16)
    xw[0] = dot32(picked, pool[...], OVER_FIRST).astype(bf16)
    target = dot32((iota((16, 512), 0) == labels[...]).astype(bf16), picked)
    by_class = [last[c].astype(f32) for c in range(CLASSES)]
    for m in range(2):
        rows = [v[m:m + 1, :] for v in by_class] + [jnp.zeros((16 - CLASSES, 512), f32)]
        last_rows[m] = jnp.concatenate(rows, axis=0).astype(bf16)
    spread_var = jnp.ones((16, 128), f32)
    for c in range(CLASSES):
        spread_var = jnp.where(iota((16, 128), 0) == c, variance[c], spread_var)
    gain = 1.0 / jnp.sqrt(spread_var)
    observed = jnp.where(core == 0, target[:, :128], target[:, 128:]) * gain

    pl.semaphore_wait(barrier, NM - 1 + 2 * (ND - 1))

    def x_copy(d):
        return pltpu.make_async_remote_copy(
            src_ref=xw.at[0], dst_ref=xw.at[d], send_sem=x_send.at[d], recv_sem=x_recv.at[d],
            device_id=(me, (y - d) % ND), device_id_type=MESH,
        )

    def give(src, dst, send_sem, recv_sem, c, t, waiting=False):
        away = (t != y) | (c != core)

        @pl.when(away)
        def _():
            copy = pltpu.make_async_remote_copy(
                src_ref=src, dst_ref=dst, send_sem=send_sem, recv_sem=recv_sem, device_id=(chip + c, t), device_id_type=MESH
            )
            if waiting:
                copy.wait_send()
            else:
                copy.start()

        if not waiting:
            @pl.when(jnp.logical_not(away))
            def _():
                pltpu.make_async_copy(src, dst, recv_sem).start()

    def give_first(waiting):
        for m in range(2):
            t = 2 * core + m
            slot = (y - t) % ND
            for c in range(2):
                give(first.at[m], wf.at[slot], f_send.at[m, c], f_recv.at[slot], c, t, waiting)
            give(last_rows.at[m], lt.at[y % 2], t_send.at[m], t_recv.at[y % 2], y // 2, t, waiting)

    def give_middle(waiting):
        for half in range(2):
            for m in range(2):
                t = 2 * core + m
                slot = (y - t) % ND
                for c in range(2):
                    src = middle.at[m, :, pl.ds(c * 1024 + half * 512, 512)]
                    give(src, mc.at[half, slot], m_send.at[half, m, c], m_recv.at[half, slot], c, t, waiting)

    for d in (2, 1, 3):
        x_copy(d).start()
    give_first(False)
    give_middle(False)

    def exchange(p, remote):
        mr, mcol = middle_block(p)
        fr, fcol = first_block(p)
        jobs = (
            (middle.at[:, mr, mcol], theta.at[pair(me), :, pl.ds(0, WIDE)]),
            (first.at[:, fr, fcol], theta.at[pair(me), :, pl.ds(WIDE, SLIM)]),
        )
        for src, dst in jobs:
            if remote:
                pltpu.make_async_remote_copy(
                    src_ref=src, dst_ref=dst, send_sem=a_send, recv_sem=a_recv, device_id=(p, y), device_id_type=MESH
                ).start()
            else:
                pltpu.make_async_copy(src, dst, a_recv).start()

    def send_one(step, carry):
        turn = (step // 8 + 2) % 8
        p = ((z + swing(step % 8)) % 8) * 8 + ((x + turn // 2) % 4) * 2 + (core + turn) % 2

        @pl.when(p != me)
        def _():
            exchange(p, True)

        @pl.when(p == me)
        def _():
            exchange(p, False)

        return carry

    def send_some(first_step, last_step):
        lax.fori_loop(first_step, last_step, send_one, 0)

    send_some(0, CUTS[0])
    for t in range(4):
        owner = 3 + 17 * t
        src = last_rows.at[:, :, pl.ds(t * 128, 128)]

        @pl.when(me == owner)
        def _():
            pltpu.make_async_copy(src, theta_last.at[pair(me)], l_recv).start()

        @pl.when(me != owner)
        def _():
            pltpu.make_async_remote_copy(
                src_ref=src, dst_ref=theta_last.at[pair(me)], send_sem=l_send.at[t], recv_sem=l_recv,
                device_id=(owner, y), device_id_type=MESH,
            ).start()

    in_scale = F_IN ** (-0.5)
    hid_scale = H ** (-0.5)
    order = (0, 1, 3, 2)
    for d in (1, 3, 2):
        x_copy(d).wait_recv()
    for d in order:
        whole_wait(wf.at[d], f_recv.at[d])

        def rows_one(i, carry, d=d):
            rows = pl.ds(pl.multiple_of(i * 256, 256), 256)
            h1[d, rows, :] = jnp.tanh(dot32(xw[i], wf[d]) * in_scale).astype(bf16)
            return carry

        lax.fori_loop(0, 4, rows_one, 0)
    for s in range(2):
        whole_wait(lt.at[s], t_recv.at[s])
    for half in range(2):
        for n, d in enumerate(order):
            whole_wait(mc.at[half, d], m_recv.at[half, d])

            def rows_two(i, carry, d=d, n=n, half=half):
                rows = pl.ds(pl.multiple_of(i * 256, 256), 256)
                term = dot32(h1[d, rows, :], mc[half, d])
                if n == 0:
                    acc[rows, :] = term
                elif n < ND - 1:
                    acc[rows, :] += term
                else:
                    h2 = jnp.tanh((acc[rows, :] + term) * hid_scale).astype(bf16)
                    here = dot32(lt[half], h2, OVER_LAST)
                    for c in range(2):
                        piece = here[:, c * 128:(c + 1) * 128]
                        if half == 0:
                            part[i, c] = piece
                        else:
                            part[i, c] += piece
                return carry

            lax.fori_loop(0, 4, rows_two, 0)

    mine = core * ND + y
    def part_copy(d, c):
        return pltpu.make_async_remote_copy(
            src_ref=part.at[d, c], dst_ref=part_in.at[mine], send_sem=p_send, recv_sem=p_recv,
            device_id=(chip + c, (y + d) % ND), device_id_type=MESH,
        )

    for c in range(2):
        for d in range(ND):
            if d == 0:
                @pl.when(core != c)
                def _():
                    part_copy(0, c).start()

                @pl.when(core == c)
                def _():
                    part_in[mine] = part[0, c]
            else:
                part_copy(d, c).start()
    send_some(CUTS[0], CUTS[1])
    whole_wait(part_in.at[pl.ds(0, 7)], p_recv)
    scaled = [((part_in[s] + part_in[ND + s]) * hid_scale * gain)[:CLASSES] for s in range(ND)]
    every[x * 8 + z] = jnp.concatenate(scaled, axis=0)

    def spread(phase, first_slot, count, p):
        slots = every.at[pl.ds(first_slot, count)]
        return pltpu.make_async_remote_copy(
            src_ref=slots, dst_ref=slots, send_sem=s_send.at[phase], recv_sem=s_recv.at[phase],
            device_id=(p, y), device_id_type=MESH,
        )

    for i in (4, 3, 5, 2, 6, 1, 7):
        spread(0, x * 8 + z, 1, ((z + i) % 8) * 8 + x * 2 + core).start()
    send_some(CUTS[1], CUTS[2])
    whole_wait(every.at[pl.ds(0, 7)], s_recv.at[0])
    for i in (2, 1, 3):
        spread(1, pl.multiple_of(x * 8, 8), 8, z * 8 + ((x + i) % 4) * 2 + core).start()
    send_some(CUTS[2], CUTS[3])
    whole_wait(every.at[pl.ds(0, 24)], s_recv.at[1])

    pull = jnp.zeros((ENS, 128), f32)
    for c in range(CLASSES):
        values = jnp.concatenate([every[:, s * CLASSES + c, :] for s in range(ND)], axis=0)
        center = jnp.mean(values, axis=0, keepdims=True)
        anomaly = values - center
        upper = anomaly.astype(bf16)
        hi_part[:, c * 128:(c + 1) * 128] = upper
        lo_part[:, c * 128:(c + 1) * 128] = (anomaly - upper.astype(f32)).astype(bf16)
        pull = pull + anomaly * (observed[c:c + 1, :] - center)
    squares = dot32(hi_part[...], hi_part[...], OVER_LAST)
    crossed = dot32(hi_part[...], lo_part[...], OVER_LAST)
    gram[:ENS, :] = squares + (crossed + crossed.T)
    drive_tall = jnp.broadcast_to(jnp.sum(pull, axis=1, keepdims=True), (ENS, ENS))
    gram[ENS:, :] = drive_tall.T[:8, :]

    def gram_copy(k):
        dc, dy = k // ND, k % ND
        return pltpu.make_async_remote_copy(
            src_ref=gram, dst_ref=gram_in.at[k - 1], send_sem=g_send, recv_sem=g_recv,
            device_id=(chip + (core + dc) % 2, (y + dy) % ND), device_id_type=MESH,
        )

    for k in (2, 6, 1, 3, 5, 7, 4):
        gram_copy(k).start()
    send_some(CUTS[3], NM)
    whole_wait(gram_in, g_recv)
    summed = gram[...]
    for k in range(7):
        summed = summed + gram_in[k]
    diagonal = iota((ENS, ENS), 0) == iota((ENS, ENS), 1)
    inverse = spd_inverse(summed[:ENS] + jnp.where(diagonal, float(ENS), 0.0))
    lift = jnp.sum(inverse * summed[ENS:ENS + 1], axis=1, keepdims=True)
    mix_t = (
        float(ENS) * (inverse - jnp.mean(inverse, axis=0, keepdims=True))
        + (lift - jnp.mean(lift, axis=0, keepdims=True))
        + 1.0 / ENS
    )
    upper = mix_t.astype(bf16)
    size = ENS * TILE
    natural = (iota((ENS, ENS), 0) == member_of_slot(iota((ENS, ENS), 1))).astype(bf16)
    mix_hi[...] = dot32(natural, upper).astype(bf16)
    mix_lo[...] = dot32(natural, (mix_t - upper.astype(f32)).astype(bf16)).astype(bf16)

    whole_wait(theta, a_recv)
    is_owner = (me - 3) % 17 == 0
    my_tile = pl.ds(pl.multiple_of(((me + 14) // 17 - 1) % 4 * 128, 128), 128)

    @pl.when(is_owner)
    def _():
        whole_wait(theta_last, l_recv)

    mr, mcol = middle_block(me)
    fr, fcol = first_block(me)

    def results(slot, p, remote):
        jobs = (
            (out.at[pair(slot), :, pl.ds(0, WIDE)], new_middle.at[:, mr, mcol], um_recv),
            (out.at[pair(slot), :, pl.ds(WIDE, SLIM)], new_first.at[:, fr, fcol], uf_recv),
        )
        for src, dst, sem in jobs:
            if remote:
                pltpu.make_async_remote_copy(
                    src_ref=src, dst_ref=dst, send_sem=u_send, recv_sem=sem, device_id=(p, y), device_id_type=MESH
                ).start()
            else:
                pltpu.make_async_copy(src, dst, sem).start()

        @pl.when(is_owner)
        def _():
            src, dst = out_last.at[pair(slot)], new_last.at[:, :, my_tile]
            if remote:
                pltpu.make_async_remote_copy(
                    src_ref=src, dst_ref=dst, send_sem=ul_send, recv_sem=ul_recv, device_id=(p, y), device_id_type=MESH
                ).start()
            else:
                pltpu.make_async_copy(src, dst, ul_recv).start()

    block = 256

    def one_block(b, carry):
        low = (me % 8 + b) % 8
        k = iota((block, ENS), 0) // TILE
        member = ((k // 2) * 8 + low) * 2 + k % 2
        choose = (member == member_of_slot(iota((block, ENS), 1))).astype(bf16)
        repeat = (iota((ENS, size), 0) == iota((ENS, size), 1) // TILE).astype(bf16)
        keep = (iota((block, size), 0) % TILE) == (iota((block, size), 1) % TILE)
        for source, wide in ((mix_hi, wide_hi), (mix_lo, wide_lo)):
            tall = dot32(choose, source[...], OVER_LAST).astype(bf16)
            wide[...] = jnp.where(keep, dot32(tall, repeat), 0.0).astype(bf16)
        flat = theta[...].reshape(size, WIDE + SLIM)
        mixed = dot32(wide_hi[...], flat) + dot32(wide_lo[...], flat)
        here = pl.ds(pl.multiple_of(b * 16, 16), 16)
        out[here] = mixed.astype(bf16).reshape(16, TILE, WIDE + SLIM)

        @pl.when(is_owner)
        def _():
            tiles = theta_last[...].reshape(size, SLIM)
            done = dot32(wide_hi[...], tiles) + dot32(wide_lo[...], tiles)
            out_last[here] = done.astype(bf16).reshape(16, TILE, SLIM)

        def send_result(turn, inner):
            there = (z + swing(turn)) % 8
            p = there * 8 + low
            slot = b * 8 + there

            @pl.when(p != me)
            def _():
                results(slot, p, True)

            @pl.when(p == me)
            def _():
                results(slot, p, False)

            return inner

        lax.fori_loop(0, 8, send_result, 0)
        return carry

    lax.fori_loop(0, 8, one_block, 0)

    for d in range(1, ND):
        x_copy(d).wait_send()
    give_first(True)
    give_middle(True)
    rest = pl.ds(0, ENS - 2)
    whole_wait(theta.at[rest], a_send)
    for t in range(4):
        @pl.when(me != 3 + 17 * t)
        def _():
            whole_wait(last_rows.at[:, :, pl.ds(t * 128, 128)], l_send.at[t])
    whole_wait(part_in.at[pl.ds(0, 7)], p_send)
    whole_wait(every.at[pl.ds(0, 7)], s_send.at[0])
    whole_wait(every.at[pl.ds(0, 24)], s_send.at[1])
    whole_wait(gram_in, g_send)
    whole_wait(new_middle, um_recv)
    whole_wait(new_first, uf_recv)
    whole_wait(new_last, ul_recv)
    whole_wait(out.at[rest], u_send)

    @pl.when(is_owner)
    def _():
        whole_wait(out_last.at[rest], ul_send)


def on_device(
    feature_pool, labels, sample_rows, noise_variance, first_weight, middle_weight, last_weight
):
    anyspace = pl.BlockSpec(memory_space=pl.ANY)
    vmem = pl.BlockSpec(memory_space=pltpu.VMEM)
    smem = pl.BlockSpec(memory_space=pltpu.SMEM)
    bf16, f32 = jnp.bfloat16, jnp.float32
    dma = pltpu.SemaphoreType.DMA
    new_first, new_middle, new_last = pl.pallas_call(
        kernel,
        out_shape=(
            jax.ShapeDtypeStruct(first_weight.shape, bf16),
            jax.ShapeDtypeStruct(middle_weight.shape, bf16),
            jax.ShapeDtypeStruct((2, TILE, 512), bf16),
        ),
        in_specs=[anyspace, anyspace, vmem, vmem, vmem, vmem, smem],
        out_specs=(anyspace, anyspace, anyspace),
        scratch_shapes=[
            pltpu.VMEM((ENS, TILE, WIDE + SLIM), bf16),
            pltpu.VMEM((ENS, TILE, SLIM), bf16),
            pltpu.VMEM((ND, 256, 512), bf16),
            pltpu.VMEM((2, ND, 512, 512), bf16),
            pltpu.VMEM((ND, 256, 256), bf16),
            pltpu.VMEM((ND, 1024, 512), bf16),
            pltpu.VMEM((1024, 512), f32),
            pltpu.VMEM((2, TILE, 512), bf16),
            pltpu.VMEM((2, TILE, 512), bf16),
            pltpu.VMEM((ND, 2, 16, 128), f32),
            pltpu.VMEM((2 * ND, 16, 128), f32),
            pltpu.VMEM((32, ND * CLASSES, 128), f32),
            pltpu.VMEM((ENS, CLASSES * 128), bf16),
            pltpu.VMEM((ENS, CLASSES * 128), bf16),
            pltpu.VMEM((ENS + 8, ENS), f32),
            pltpu.VMEM((7, ENS + 8, ENS), f32),
            pltpu.VMEM((ENS, ENS), bf16),
            pltpu.VMEM((ENS, ENS), bf16),
            pltpu.VMEM((256, ENS * TILE), bf16),
            pltpu.VMEM((256, ENS * TILE), bf16),
            pltpu.VMEM((ENS, TILE, WIDE + SLIM), bf16),
            pltpu.VMEM((ENS, TILE, SLIM), bf16),
            dma((ND,)), dma((ND,)),
            dma((2, 2)), dma((ND,)),
            dma((2, 2, 2)), dma((2, ND)),
            dma((2,)), dma((2,)),
            dma, dma,
            dma((4,)), dma,
            dma, dma,
            dma((2,)), dma((2,)),
            dma, dma,
            dma, dma, dma, dma, dma,
        ],
        compiler_params=pltpu.CompilerParams(collective_id=0, has_side_effects=True, vmem_limit_bytes=VMEM_LIMIT),
    )(
        first_weight, middle_weight, feature_pool, labels.reshape(1, -1), sample_rows.reshape(1, -1), jnp.transpose(last_weight, (2, 0, 1)),
        noise_variance,
    )
    new_last = jnp.swapaxes(new_last[:, :CLASSES, :], 1, 2)
    return (new_first, new_middle, new_last)


def solution(mesh):
    in_specs = (
        P("dp", None),
        P("dp"),
        P("dp"),
        P(),
        P("member", None, "dp"),
        P("member", "dp", None),
        P("member", "dp", None),
    )
    out_specs = (P("member", None, "dp"), P("member", "dp", None), P("member", "dp", None))
    return jax.shard_map(
        on_device, mesh=mesh, in_specs=in_specs, out_specs=out_specs, check_vma=False
    )
```

```python
import functools

import jax
import jax.numpy as jnp
from jax import lax
from jax.experimental import pallas as pl
from jax.experimental.pallas import tpu as pltpu
from jax.sharding import PartitionSpec as P

F_IN = 256
H = 2048
MESH = pl.DeviceIdType.MESH
NM = 64
ND = 4
ENS = 128
CLASSES = 10
CUTS = (40, 40, 40, 56)
TILE = 16
WIDE = 1024
SLIM = 128
VMEM_LIMIT = 60 * 1024 * 1024
OVER_LAST = (((1,), (1,)), ((), ()))
OVER_FIRST = (((0,), (0,)), ((), ()))


def dot32(a, b, dims=(((1,), (0,)), ((), ()))):
    return lax.dot_general(a, b, dims, preferred_element_type=jnp.float32)


def iota(shape, dim):
    return lax.broadcasted_iota(jnp.int32, shape, dim)


def middle_block(p):
    return pl.ds(pl.multiple_of((p // 2) * TILE, TILE), TILE), pl.ds(pl.multiple_of((p % 2) * WIDE, WIDE), WIDE)


def first_block(p):
    return pl.ds(pl.multiple_of((p // 4) * TILE, TILE), TILE), pl.ds(pl.multiple_of((p % 4) * SLIM, SLIM), SLIM)


def pair(p):
    return pl.ds(pl.multiple_of(2 * p, 2), 2)


def swing(turn):
    up = (turn + 1) // 2
    out = (turn % 2) * up + (1 - turn % 2) * (8 - up)
    far = (7 - turn) // 7
    return (out * (1 - far) + 4 * far - 4 * (turn // 7)) % 8


def whole_wait(ref, sem):
    pltpu.make_async_copy(ref, ref, sem).wait()


def spd_inverse(system):
    size = system.shape[0]
    group = 8
    sub = iota((group, size), 0)
    lane = iota((group, size), 1)
    lanes = iota((size - group, size), 1)

    def one_round(_, a):
        panel = a[:group, :]
        for k in range(0, group, 2):
            one, two = panel[k:k + 1, :], panel[k + 1:k + 2, :]
            col_one, col_two = panel[:, k:k + 1], panel[:, k + 1:k + 2]
            at_one, at_two = lane == k, lane == k + 1
            p, q = one[:, k:k + 1], one[:, k + 1:k + 2]
            r, t = two[:, k:k + 1], two[:, k + 1:k + 2]
            scale = 1.0 / (p * t - q * r)
            one = jnp.where(at_one[:1], 1.0, jnp.where(at_two[:1], 0.0, one))
            two = jnp.where(at_one[:1], 0.0, jnp.where(at_two[:1], 1.0, two))
            one, two = (t * one - q * two) * scale, (p * two - r * one) * scale
            rest = jnp.where(at_one | at_two, 0.0, panel) - col_one * one - col_two * two
            panel = jnp.where(sub == k, one, jnp.where(sub == k + 1, two, rest))
        below = jnp.where(lanes < group, 0.0, a[group:, :])
        for k in range(group):
            below = below - a[group:, k:k + 1] * panel[k:k + 1, :]
        turned = jnp.concatenate([below, panel], axis=0)
        return pltpu.roll(turned, size - group, 1)

    return lax.fori_loop(0, size // group, one_round, system)


def member_of_slot(i):
    return (i % 8) * 16 + ((i // 8) % 4) * 4 + i // 32


def kernel(
    first, middle, pool, labels, rows_picked, last, variance,
    new_first, new_middle, new_last,
    theta, theta_last, wf, mc, xw, h1, acc, lt, last_rows, part, part_in, every, hi_part, lo_part, gram, gram_in,
    mix_hi, mix_lo, wide_hi, wide_lo, out, out_last,
    x_send, x_recv, f_send, f_recv, m_send, m_recv, t_send, t_recv,
    a_send, a_recv, l_send, l_recv, p_send, p_recv, s_send, s_recv, g_send, g_recv,
    u_send, um_recv, uf_recv, ul_send, ul_recv,
):
    bf16, f32 = jnp.bfloat16, jnp.float32
    me, y = lax.axis_index("member"), lax.axis_index("dp")
    z, x, core = me // 8, (me // 2) % 4, me % 2
    chip = me - core
    barrier = pltpu.get_barrier_semaphore()
    for c in range(2):
        for d in range(1, ND):
            pl.semaphore_signal(barrier, inc=1, device_id=(chip + c, (y + d) % ND), device_id_type=MESH)

    def greet(i, carry):
        pl.semaphore_signal(barrier, inc=1, device_id=((me + i) % NM, y), device_id_type=MESH)
        return carry

    lax.fori_loop(1, NM, greet, 0)

    picked = (iota((512, 256), 0) == rows_picked[...]).astype(bf16)
    xw[0] = dot32(picked, pool[...], OVER_FIRST).astype(bf16)
    target = dot32((iota((16, 512), 0) == labels[...]).astype(bf16), picked)
    by_class = [last[c].astype(f32) for c in range(CLASSES)]
    for m in range(2):
        rows = [v[m:m + 1, :] for v in by_class] + [jnp.zeros((16 - CLASSES, 512), f32)]
        last_rows[m] = jnp.concatenate(rows, axis=0).astype(bf16)
    spread_var = jnp.ones((16, 128), f32)
    for c in range(CLASSES):
        spread_var = jnp.where(iota((16, 128), 0) == c, variance[c], spread_var)
    gain = 1.0 / jnp.sqrt(spread_var)
    observed = jnp.where(core == 0, target[:, :128], target[:, 128:]) * gain

    pl.semaphore_wait(barrier, NM - 1 + 2 * (ND - 1))

    def x_copy(d):
        return pltpu.make_async_remote_copy(
            src_ref=xw.at[0], dst_ref=xw.at[d], send_sem=x_send.at[d], recv_sem=x_recv.at[d],
            device_id=(me, (y - d) % ND), device_id_type=MESH,
        )

    def give(src, dst, send_sem, recv_sem, c, t, waiting=False):
        away = (t != y) | (c != core)

        @pl.when(away)
        def _():
            copy = pltpu.make_async_remote_copy(
                src_ref=src, dst_ref=dst, send_sem=send_sem, recv_sem=recv_sem, device_id=(chip + c, t), device_id_type=MESH
            )
            if waiting:
                copy.wait_send()
            else:
                copy.start()

        if not waiting:
            @pl.when(jnp.logical_not(away))
            def _():
                pltpu.make_async_copy(src, dst, recv_sem).start()

    def give_first(waiting):
        for m in range(2):
            t = 2 * core + m
            slot = (y - t) % ND
            for c in range(2):
                give(first.at[m], wf.at[slot], f_send.at[m, c], f_recv.at[slot], c, t, waiting)
            give(last_rows.at[m], lt.at[y % 2], t_send.at[m], t_recv.at[y % 2], y // 2, t, waiting)

    def give_middle(waiting):
        for half in range(2):
            for m in range(2):
                t = 2 * core + m
                slot = (y - t) % ND
                for c in range(2):
                    src = middle.at[m, :, pl.ds(c * 1024 + half * 512, 512)]
                    give(src, mc.at[half, slot], m_send.at[half, m, c], m_recv.at[half, slot], c, t, waiting)

    for d in (2, 1, 3):
        x_copy(d).start()
    give_first(False)
    give_middle(False)

    def exchange(p, remote):
        mr, mcol = middle_block(p)
        fr, fcol = first_block(p)
        jobs = (
            (middle.at[:, mr, mcol], theta.at[pair(me), :, pl.ds(0, WIDE)]),
            (first.at[:, fr, fcol], theta.at[pair(me), :, pl.ds(WIDE, SLIM)]),
        )
        for src, dst in jobs:
            if remote:
                pltpu.make_async_remote_copy(
                    src_ref=src, dst_ref=dst, send_sem=a_send, recv_sem=a_recv, device_id=(p, y), device_id_type=MESH
                ).start()
            else:
                pltpu.make_async_copy(src, dst, a_recv).start()

    def send_one(step, carry):
        turn = (step // 8 + 2) % 8
        p = ((z + swing(step % 8)) % 8) * 8 + ((x + turn // 2) % 4) * 2 + (core + turn) % 2

        @pl.when(p != me)
        def _():
            exchange(p, True)

        @pl.when(p == me)
        def _():
            exchange(p, False)

        return carry

    def send_some(first_step, last_step):
        lax.fori_loop(first_step, last_step, send_one, 0)

    send_some(0, CUTS[0])
    for t in range(4):
        owner = 3 + 17 * t
        src = last_rows.at[:, :, pl.ds(t * 128, 128)]

        @pl.when(me == owner)
        def _():
            pltpu.make_async_copy(src, theta_last.at[pair(me)], l_recv).start()

        @pl.when(me != owner)
        def _():
            pltpu.make_async_remote_copy(
                src_ref=src, dst_ref=theta_last.at[pair(me)], send_sem=l_send.at[t], recv_sem=l_recv,
                device_id=(owner, y), device_id_type=MESH,
            ).start()

    in_scale = F_IN ** (-0.5)
    hid_scale = H ** (-0.5)
    order = (0, 1, 3, 2)
    for d in (1, 3, 2):
        x_copy(d).wait_recv()
    for d in order:
        whole_wait(wf.at[d], f_recv.at[d])

        def rows_one(i, carry, d=d):
            rows = pl.ds(pl.multiple_of(i * 256, 256), 256)
            h1[d, rows, :] = jnp.tanh(dot32(xw[i], wf[d]) * in_scale).astype(bf16)
            return carry

        lax.fori_loop(0, 4, rows_one, 0)
    for s in range(2):
        whole_wait(lt.at[s], t_recv.at[s])
    for half in range(2):
        for n, d in enumerate(order):
            whole_wait(mc.at[half, d], m_recv.at[half, d])

            def rows_two(i, carry, d=d, n=n, half=half):
                rows = pl.ds(pl.multiple_of(i * 256, 256), 256)
                term = dot32(h1[d, rows, :], mc[half, d])
                if n == 0:
                    acc[rows, :] = term
                elif n < ND - 1:
                    acc[rows, :] += term
                else:
                    h2 = jnp.tanh((acc[rows, :] + term) * hid_scale).astype(bf16)
                    here = dot32(lt[half], h2, OVER_LAST)
                    for c in range(2):
                        piece = here[:, c * 128:(c + 1) * 128]
                        if half == 0:
                            part[i, c] = piece
                        else:
                            part[i, c] += piece
                return carry

            lax.fori_loop(0, 4, rows_two, 0)

    mine = core * ND + y
    def part_copy(d, c):
        return pltpu.make_async_remote_copy(
            src_ref=part.at[d, c], dst_ref=part_in.at[mine], send_sem=p_send, recv_sem=p_recv,
            device_id=(chip + c, (y + d) % ND), device_id_type=MESH,
        )

    for c in range(2):
        for d in range(ND):
            if d == 0:
                @pl.when(core != c)
                def _():
                    part_copy(0, c).start()

                @pl.when(core == c)
                def _():
                    part_in[mine] = part[0, c]
            else:
                part_copy(d, c).start()
    send_some(CUTS[0], CUTS[1])
    whole_wait(part_in.at[pl.ds(0, 7)], p_recv)
    scaled = [((part_in[s] + part_in[ND + s]) * hid_scale * gain)[:CLASSES] for s in range(ND)]
    every[x * 8 + z] = jnp.concatenate(scaled, axis=0)

    def spread(phase, first_slot, count, p):
        slots = every.at[pl.ds(first_slot, count)]
        return pltpu.make_async_remote_copy(
            src_ref=slots, dst_ref=slots, send_sem=s_send.at[phase], recv_sem=s_recv.at[phase],
            device_id=(p, y), device_id_type=MESH,
        )

    for i in (4, 3, 5, 2, 6, 1, 7):
        spread(0, x * 8 + z, 1, ((z + i) % 8) * 8 + x * 2 + core).start()
    send_some(CUTS[1], CUTS[2])
    whole_wait(every.at[pl.ds(0, 7)], s_recv.at[0])
    for i in (2, 1, 3):
        spread(1, pl.multiple_of(x * 8, 8), 8, z * 8 + ((x + i) % 4) * 2 + core).start()
    send_some(CUTS[2], CUTS[3])
    whole_wait(every.at[pl.ds(0, 24)], s_recv.at[1])

    pull = jnp.zeros((ENS, 128), f32)
    for c in range(CLASSES):
        values = jnp.concatenate([every[:, s * CLASSES + c, :] for s in range(ND)], axis=0)
        center = jnp.mean(values, axis=0, keepdims=True)
        anomaly = values - center
        upper = anomaly.astype(bf16)
        hi_part[:, c * 128:(c + 1) * 128] = upper
        lo_part[:, c * 128:(c + 1) * 128] = (anomaly - upper.astype(f32)).astype(bf16)
        pull = pull + anomaly * (observed[c:c + 1, :] - center)
    squares = dot32(hi_part[...], hi_part[...], OVER_LAST)
    crossed = dot32(hi_part[...], lo_part[...], OVER_LAST)
    gram[:ENS, :] = squares + (crossed + crossed.T)
    drive_tall = jnp.broadcast_to(jnp.sum(pull, axis=1, keepdims=True), (ENS, ENS))
    gram[ENS:, :] = drive_tall.T[:8, :]

    def gram_copy(k):
        dc, dy = k // ND, k % ND
        return pltpu.make_async_remote_copy(
            src_ref=gram, dst_ref=gram_in.at[k - 1], send_sem=g_send, recv_sem=g_recv,
            device_id=(chip + (core + dc) % 2, (y + dy) % ND), device_id_type=MESH,
        )

    for k in (2, 6, 1, 3, 5, 7, 4):
        gram_copy(k).start()
    send_some(CUTS[3], NM)
    whole_wait(gram_in, g_recv)
    summed = gram[...]
    for k in range(7):
        summed = summed + gram_in[k]
    diagonal = iota((ENS, ENS), 0) == iota((ENS, ENS), 1)
    inverse = spd_inverse(summed[:ENS] + jnp.where(diagonal, float(ENS), 0.0))
    lift = jnp.sum(inverse * summed[ENS:ENS + 1], axis=1, keepdims=True)
    mix_t = (
        float(ENS) * (inverse - jnp.mean(inverse, axis=0, keepdims=True))
        + (lift - jnp.mean(lift, axis=0, keepdims=True))
        + 1.0 / ENS
    )
    upper = mix_t.astype(bf16)
    size = ENS * TILE
    natural = (iota((ENS, ENS), 0) == member_of_slot(iota((ENS, ENS), 1))).astype(bf16)
    mix_hi[...] = dot32(natural, upper).astype(bf16)
    mix_lo[...] = dot32(natural, (mix_t - upper.astype(f32)).astype(bf16)).astype(bf16)

    whole_wait(theta, a_recv)
    is_owner = (me - 3) % 17 == 0
    my_tile = pl.ds(pl.multiple_of(((me + 14) // 17 - 1) % 4 * 128, 128), 128)

    @pl.when(is_owner)
    def _():
        whole_wait(theta_last, l_recv)

    mr, mcol = middle_block(me)
    fr, fcol = first_block(me)

    def results(slot, p, remote):
        jobs = (
            (out.at[pair(slot), :, pl.ds(0, WIDE)], new_middle.at[:, mr, mcol], um_recv),
            (out.at[pair(slot), :, pl.ds(WIDE, SLIM)], new_first.at[:, fr, fcol], uf_recv),
        )
        for src, dst, sem in jobs:
            if remote:
                pltpu.make_async_remote_copy(
                    src_ref=src, dst_ref=dst, send_sem=u_send, recv_sem=sem, device_id=(p, y), device_id_type=MESH
                ).start()
            else:
                pltpu.make_async_copy(src, dst, sem).start()

        @pl.when(is_owner)
        def _():
            src, dst = out_last.at[pair(slot)], new_last.at[:, :, my_tile]
            if remote:
                pltpu.make_async_remote_copy(
                    src_ref=src, dst_ref=dst, send_sem=ul_send, recv_sem=ul_recv, device_id=(p, y), device_id_type=MESH
                ).start()
            else:
                pltpu.make_async_copy(src, dst, ul_recv).start()

    block = 256

    def one_block(b, carry):
        low = (me % 8 + b) % 8
        k = iota((block, ENS), 0) // TILE
        member = ((k // 2) * 8 + low) * 2 + k % 2
        choose = (member == member_of_slot(iota((block, ENS), 1))).astype(bf16)
        repeat = (iota((ENS, size), 0) == iota((ENS, size), 1) // TILE).astype(bf16)
        keep = (iota((block, size), 0) % TILE) == (iota((block, size), 1) % TILE)
        for source, wide in ((mix_hi, wide_hi), (mix_lo, wide_lo)):
            tall = dot32(choose, source[...], OVER_LAST).astype(bf16)
            wide[...] = jnp.where(keep, dot32(tall, repeat), 0.0).astype(bf16)
        flat = theta[...].reshape(size, WIDE + SLIM)
        mixed = dot32(wide_hi[...], flat) + dot32(wide_lo[...], flat)
        here = pl.ds(pl.multiple_of(b * 16, 16), 16)
        out[here] = mixed.astype(bf16).reshape(16, TILE, WIDE + SLIM)

        @pl.when(is_owner)
        def _():
            tiles = theta_last[...].reshape(size, SLIM)
            done = dot32(wide_hi[...], tiles) + dot32(wide_lo[...], tiles)
            out_last[here] = done.astype(bf16).reshape(16, TILE, SLIM)

        def send_result(turn, inner):
            there = (z + swing(turn)) % 8
            p = there * 8 + low
            slot = b * 8 + there

            @pl.when(p != me)
            def _():
                results(slot, p, True)

            @pl.when(p == me)
            def _():
                results(slot, p, False)

            return inner

        lax.fori_loop(0, 8, send_result, 0)
        return carry

    lax.fori_loop(0, 8, one_block, 0)

    for d in range(1, ND):
        x_copy(d).wait_send()
    give_first(True)
    give_middle(True)
    rest = pl.ds(0, ENS - 2)
    whole_wait(theta.at[rest], a_send)
    for t in range(4):
        @pl.when(me != 3 + 17 * t)
        def _():
            whole_wait(last_rows.at[:, :, pl.ds(t * 128, 128)], l_send.at[t])
    whole_wait(part_in.at[pl.ds(0, 7)], p_send)
    whole_wait(every.at[pl.ds(0, 7)], s_send.at[0])
    whole_wait(every.at[pl.ds(0, 24)], s_send.at[1])
    whole_wait(gram_in, g_send)
    whole_wait(new_middle, um_recv)
    whole_wait(new_first, uf_recv)
    whole_wait(new_last, ul_recv)
    whole_wait(out.at[rest], u_send)

    @pl.when(is_owner)
    def _():
        whole_wait(out_last.at[rest], ul_send)


def settle(middle, first, settled_middle, settled_first, held_middle, held_first, in_sems, out_sems):
    steps = []
    for m in range(2):
        for k in range(4):
            at = (m, pl.ds(k * 128, 128))
            steps.append((middle.at[at], held_middle.at[at], settled_middle.at[at], in_sems.at[m, k], out_sems.at[m, k]))
        steps.append((first.at[m], held_first.at[m], settled_first.at[m], in_sems.at[m, 4], out_sems.at[m, 4]))
    ins = [pltpu.make_async_copy(src, held, sem) for src, held, _, sem, _ in steps]
    outs = [pltpu.make_async_copy(held, dst, sem) for _, held, dst, _, sem in steps]
    for copy in ins:
        copy.start()
    for came, goes in zip(ins, outs):
        came.wait()
        goes.start()
    for copy in outs:
        copy.wait()


def on_device(
    feature_pool, labels, sample_rows, noise_variance, first_weight, middle_weight, last_weight
):
    anyspace = pl.BlockSpec(memory_space=pl.ANY)
    vmem = pl.BlockSpec(memory_space=pltpu.VMEM)
    smem = pl.BlockSpec(memory_space=pltpu.SMEM)
    bf16, f32 = jnp.bfloat16, jnp.float32
    dma = pltpu.SemaphoreType.DMA
    new_first, new_middle, new_last = pl.pallas_call(
        kernel,
        out_shape=(
            jax.ShapeDtypeStruct(first_weight.shape, bf16),
            jax.ShapeDtypeStruct(middle_weight.shape, bf16),
            jax.ShapeDtypeStruct((2, TILE, 512), bf16),
        ),
        in_specs=[anyspace, anyspace, vmem, vmem, vmem, vmem, smem],
        out_specs=(anyspace, anyspace, anyspace),
        scratch_shapes=[
            pltpu.VMEM((ENS, TILE, WIDE + SLIM), bf16),
            pltpu.VMEM((ENS, TILE, SLIM), bf16),
            pltpu.VMEM((ND, 256, 512), bf16),
            pltpu.VMEM((2, ND, 512, 512), bf16),
            pltpu.VMEM((ND, 256, 256), bf16),
            pltpu.VMEM((ND, 1024, 512), bf16),
            pltpu.VMEM((1024, 512), f32),
            pltpu.VMEM((2, TILE, 512), bf16),
            pltpu.VMEM((2, TILE, 512), bf16),
            pltpu.VMEM((ND, 2, 16, 128), f32),
            pltpu.VMEM((2 * ND, 16, 128), f32),
            pltpu.VMEM((32, ND * CLASSES, 128), f32),
            pltpu.VMEM((ENS, CLASSES * 128), bf16),
            pltpu.VMEM((ENS, CLASSES * 128), bf16),
            pltpu.VMEM((ENS + 8, ENS), f32),
            pltpu.VMEM((7, ENS + 8, ENS), f32),
            pltpu.VMEM((ENS, ENS), bf16),
            pltpu.VMEM((ENS, ENS), bf16),
            pltpu.VMEM((256, ENS * TILE), bf16),
            pltpu.VMEM((256, ENS * TILE), bf16),
            pltpu.VMEM((ENS, TILE, WIDE + SLIM), bf16),
            pltpu.VMEM((ENS, TILE, SLIM), bf16),
            dma((ND,)), dma((ND,)),
            dma((2, 2)), dma((ND,)),
            dma((2, 2, 2)), dma((2, ND)),
            dma((2,)), dma((2,)),
            dma, dma,
            dma((4,)), dma,
            dma, dma,
            dma((2,)), dma((2,)),
            dma, dma,
            dma, dma, dma, dma, dma,
        ],
        compiler_params=pltpu.CompilerParams(collective_id=0, has_side_effects=True, vmem_limit_bytes=VMEM_LIMIT),
    )(
        first_weight, middle_weight, feature_pool, labels.reshape(1, -1), sample_rows.reshape(1, -1), jnp.transpose(last_weight, (2, 0, 1)),
        noise_variance,
    )
    new_middle, new_first = pl.pallas_call(
        settle,
        out_shape=(
            jax.ShapeDtypeStruct(middle_weight.shape, bf16),
            jax.ShapeDtypeStruct(first_weight.shape, bf16),
        ),
        in_specs=[anyspace, anyspace],
        out_specs=(anyspace, anyspace),
        scratch_shapes=[
            pltpu.VMEM(middle_weight.shape, bf16), pltpu.VMEM(first_weight.shape, bf16), dma((2, 5)), dma((2, 5)),
        ],
        compiler_params=pltpu.CompilerParams(vmem_limit_bytes=VMEM_LIMIT),
    )(new_middle, new_first)
    new_last = jnp.swapaxes(new_last[:, :CLASSES, :], 1, 2)
    return (new_first, new_middle, new_last)


def solution(mesh):
    in_specs = (
        P("dp", None),
        P("dp"),
        P("dp"),
        P(),
        P("member", None, "dp"),
        P("member", "dp", None),
        P("member", "dp", None),
    )
    out_specs = (P("member", None, "dp"), P("member", "dp", None), P("member", "dp", None))
    return jax.shard_map(
        on_device, mesh=mesh, in_specs=in_specs, out_specs=out_specs, check_vma=False
    )
```

```python
import functools

import jax
import jax.numpy as jnp
from jax import lax
from jax.experimental import pallas as pl
from jax.experimental.pallas import tpu as pltpu
from jax.sharding import PartitionSpec as P

F_IN = 256
H = 2048
MESH = pl.DeviceIdType.MESH
NM = 64
ND = 4
ENS = 128
CLASSES = 10
CUTS = (42, 42, 42, 56)
TILE = 16
WIDE = 1024
SLIM = 128
VMEM_LIMIT = 60 * 1024 * 1024
OVER_LAST = (((1,), (1,)), ((), ()))
OVER_FIRST = (((0,), (0,)), ((), ()))


def dot32(a, b, dims=(((1,), (0,)), ((), ()))):
    return lax.dot_general(a, b, dims, preferred_element_type=jnp.float32)


def iota(shape, dim):
    return lax.broadcasted_iota(jnp.int32, shape, dim)


def middle_block(p):
    return pl.ds(pl.multiple_of((p // 2) * TILE, TILE), TILE), pl.ds(pl.multiple_of((p % 2) * WIDE, WIDE), WIDE)


def first_block(p):
    return pl.ds(pl.multiple_of((p // 4) * TILE, TILE), TILE), pl.ds(pl.multiple_of((p % 4) * SLIM, SLIM), SLIM)


def pair(p):
    return pl.ds(pl.multiple_of(2 * p, 2), 2)


def swing(turn):
    up = (turn + 1) // 2
    out = (turn % 2) * up + (1 - turn % 2) * (8 - up)
    far = (7 - turn) // 7
    return (out * (1 - far) + 4 * far - 4 * (turn // 7)) % 8


def whole_wait(ref, sem):
    pltpu.make_async_copy(ref, ref, sem).wait()


def spd_inverse(system):
    size = system.shape[0]
    group = 8
    sub = iota((group, size), 0)
    lane = iota((group, size), 1)
    lanes = iota((size - group, size), 1)

    def one_round(_, a):
        panel = a[:group, :]
        for k in range(0, group, 2):
            one, two = panel[k:k + 1, :], panel[k + 1:k + 2, :]
            col_one, col_two = panel[:, k:k + 1], panel[:, k + 1:k + 2]
            at_one, at_two = lane == k, lane == k + 1
            p, q = one[:, k:k + 1], one[:, k + 1:k + 2]
            r, t = two[:, k:k + 1], two[:, k + 1:k + 2]
            scale = 1.0 / (p * t - q * r)
            one = jnp.where(at_one[:1], 1.0, jnp.where(at_two[:1], 0.0, one))
            two = jnp.where(at_one[:1], 0.0, jnp.where(at_two[:1], 1.0, two))
            one, two = (t * one - q * two) * scale, (p * two - r * one) * scale
            rest = jnp.where(at_one | at_two, 0.0, panel) - col_one * one - col_two * two
            panel = jnp.where(sub == k, one, jnp.where(sub == k + 1, two, rest))
        below = jnp.where(lanes < group, 0.0, a[group:, :])
        for k in range(group):
            below = below - a[group:, k:k + 1] * panel[k:k + 1, :]
        turned = jnp.concatenate([below, panel], axis=0)
        return pltpu.roll(turned, size - group, 1)

    return lax.fori_loop(0, size // group, one_round, system)


def member_of_slot(i):
    return (i % 8) * 16 + ((i // 8) % 4) * 4 + i // 32


def kernel(
    first, middle, pool, labels, rows_picked, last, variance,
    new_first, new_middle, new_last,
    theta, theta_last, wf, mc, xw, h1, acc, lt, last_rows, part, part_in, every, hi_part, lo_part, gram, gram_in,
    mix_hi, mix_lo, wide_hi, wide_lo, out, out_last,
    x_send, x_recv, f_send, f_recv, m_send, m_recv, t_send, t_recv,
    a_send, a_recv, l_send, l_recv, p_send, p_recv, s_send, s_recv, g_send, g_recv,
    u_send, um_recv, uf_recv, ul_send, ul_recv,
):
    bf16, f32 = jnp.bfloat16, jnp.float32
    me, y = lax.axis_index("member"), lax.axis_index("dp")
    z, x, core = me // 8, (me // 2) % 4, me % 2
    chip = me - core
    barrier = pltpu.get_barrier_semaphore()
    for c in range(2):
        for d in range(1, ND):
            pl.semaphore_signal(barrier, inc=1, device_id=(chip + c, (y + d) % ND), device_id_type=MESH)

    def greet(i, carry):
        pl.semaphore_signal(barrier, inc=1, device_id=((me + i) % NM, y), device_id_type=MESH)
        return carry

    lax.fori_loop(1, NM, greet, 0)

    picked = (iota((512, 256), 0) == rows_picked[...]).astype(bf16)
    xw[0] = dot32(picked, pool[...], OVER_FIRST).astype(bf16)
    target = dot32((iota((16, 512), 0) == labels[...]).astype(bf16), picked)
    by_class = [last[c].astype(f32) for c in range(CLASSES)]
    for m in range(2):
        rows = [v[m:m + 1, :] for v in by_class] + [jnp.zeros((16 - CLASSES, 512), f32)]
        last_rows[m] = jnp.concatenate(rows, axis=0).astype(bf16)
    spread_var = jnp.ones((16, 128), f32)
    for c in range(CLASSES):
        spread_var = jnp.where(iota((16, 128), 0) == c, variance[c], spread_var)
    gain = 1.0 / jnp.sqrt(spread_var)
    observed = jnp.where(core == 0, target[:, :128], target[:, 128:]) * gain

    pl.semaphore_wait(barrier, NM - 1 + 2 * (ND - 1))

    def x_copy(d):
        return pltpu.make_async_remote_copy(
            src_ref=xw.at[0], dst_ref=xw.at[d], send_sem=x_send.at[d], recv_sem=x_recv.at[d],
            device_id=(me, (y - d) % ND), device_id_type=MESH,
        )

    def give(src, dst, send_sem, recv_sem, c, t, waiting=False):
        away = (t != y) | (c != core)

        @pl.when(away)
        def _():
            copy = pltpu.make_async_remote_copy(
                src_ref=src, dst_ref=dst, send_sem=send_sem, recv_sem=recv_sem, device_id=(chip + c, t), device_id_type=MESH
            )
            if waiting:
                copy.wait_send()
            else:
                copy.start()

        if not waiting:
            @pl.when(jnp.logical_not(away))
            def _():
                pltpu.make_async_copy(src, dst, recv_sem).start()

    def give_first(waiting):
        for m in range(2):
            t = 2 * core + m
            slot = (y - t) % ND
            for c in range(2):
                give(first.at[m], wf.at[slot], f_send.at[m, c], f_recv.at[slot], c, t, waiting)
            give(last_rows.at[m], lt.at[y % 2], t_send.at[m], t_recv.at[y % 2], y // 2, t, waiting)

    def give_middle(waiting):
        for half in range(2):
            for m in range(2):
                t = 2 * core + m
                slot = (y - t) % ND
                for c in range(2):
                    src = middle.at[m, :, pl.ds(c * 1024 + half * 512, 512)]
                    give(src, mc.at[half, slot], m_send.at[half, m, c], m_recv.at[half, slot], c, t, waiting)

    for d in (2, 1, 3):
        x_copy(d).start()
    give_first(False)
    give_middle(False)

    def exchange(p, remote):
        mr, mcol = middle_block(p)
        fr, fcol = first_block(p)
        jobs = (
            (middle.at[:, mr, mcol], theta.at[pair(me), :, pl.ds(0, WIDE)]),
            (first.at[:, fr, fcol], theta.at[pair(me), :, pl.ds(WIDE, SLIM)]),
        )
        for src, dst in jobs:
            if remote:
                pltpu.make_async_remote_copy(
                    src_ref=src, dst_ref=dst, send_sem=a_send, recv_sem=a_recv, device_id=(p, y), device_id_type=MESH
                ).start()
            else:
                pltpu.make_async_copy(src, dst, a_recv).start()

    def send_one(step, carry):
        turn = (step // 8 + 2) % 8
        p = ((z + swing(step % 8)) % 8) * 8 + ((x + turn // 2) % 4) * 2 + (core + turn) % 2

        @pl.when(p != me)
        def _():
            exchange(p, True)

        @pl.when(p == me)
        def _():
            exchange(p, False)

        return carry

    def send_some(first_step, last_step):
        lax.fori_loop(first_step, last_step, send_one, 0)

    send_some(0, CUTS[0])
    for t in range(4):
        owner = 3 + 17 * t
        src = last_rows.at[:, :, pl.ds(t * 128, 128)]

        @pl.when(me == owner)
        def _():
            pltpu.make_async_copy(src, theta_last.at[pair(me)], l_recv).start()

        @pl.when(me != owner)
        def _():
            pltpu.make_async_remote_copy(
                src_ref=src, dst_ref=theta_last.at[pair(me)], send_sem=l_send.at[t], recv_sem=l_recv,
                device_id=(owner, y), device_id_type=MESH,
            ).start()

    in_scale = F_IN ** (-0.5)
    hid_scale = H ** (-0.5)
    order = (0, 1, 3, 2)
    for d in (1, 3, 2):
        x_copy(d).wait_recv()
    for d in order:
        whole_wait(wf.at[d], f_recv.at[d])

        def rows_one(i, carry, d=d):
            rows = pl.ds(pl.multiple_of(i * 256, 256), 256)
            h1[d, rows, :] = jnp.tanh(dot32(xw[i], wf[d]) * in_scale).astype(bf16)
            return carry

        lax.fori_loop(0, 4, rows_one, 0)
    for s in range(2):
        whole_wait(lt.at[s], t_recv.at[s])
    for half in range(2):
        for n, d in enumerate(order):
            whole_wait(mc.at[half, d], m_recv.at[half, d])

            def rows_two(i, carry, d=d, n=n, half=half):
                rows = pl.ds(pl.multiple_of(i * 256, 256), 256)
                term = dot32(h1[d, rows, :], mc[half, d])
                if n == 0:
                    acc[rows, :] = term
                elif n < ND - 1:
                    acc[rows, :] += term
                else:
                    h2 = jnp.tanh((acc[rows, :] + term) * hid_scale).astype(bf16)
                    here = dot32(lt[half], h2, OVER_LAST)
                    for c in range(2):
                        piece = here[:, c * 128:(c + 1) * 128]
                        if half == 0:
                            part[i, c] = piece
                        else:
                            part[i, c] += piece
                return carry

            lax.fori_loop(0, 4, rows_two, 0)

    mine = core * ND + y
    def part_copy(d, c):
        return pltpu.make_async_remote_copy(
            src_ref=part.at[d, c], dst_ref=part_in.at[mine], send_sem=p_send, recv_sem=p_recv,
            device_id=(chip + c, (y + d) % ND), device_id_type=MESH,
        )

    for c in range(2):
        for d in range(ND):
            if d == 0:
                @pl.when(core != c)
                def _():
                    part_copy(0, c).start()

                @pl.when(core == c)
                def _():
                    part_in[mine] = part[0, c]
            else:
                part_copy(d, c).start()
    send_some(CUTS[0], CUTS[1])
    whole_wait(part_in.at[pl.ds(0, 7)], p_recv)
    scaled = [((part_in[s] + part_in[ND + s]) * hid_scale * gain)[:CLASSES] for s in range(ND)]
    every[x * 8 + z] = jnp.concatenate(scaled, axis=0)

    def spread(phase, first_slot, count, p):
        slots = every.at[pl.ds(first_slot, count)]
        return pltpu.make_async_remote_copy(
            src_ref=slots, dst_ref=slots, send_sem=s_send.at[phase], recv_sem=s_recv.at[phase],
            device_id=(p, y), device_id_type=MESH,
        )

    for i in (4, 3, 5, 2, 6, 1, 7):
        spread(0, x * 8 + z, 1, ((z + i) % 8) * 8 + x * 2 + core).start()
    send_some(CUTS[1], CUTS[2])
    whole_wait(every.at[pl.ds(0, 7)], s_recv.at[0])
    for i in (2, 1, 3):
        spread(1, pl.multiple_of(x * 8, 8), 8, z * 8 + ((x + i) % 4) * 2 + core).start()
    send_some(CUTS[2], CUTS[3])
    whole_wait(every.at[pl.ds(0, 24)], s_recv.at[1])

    pull = jnp.zeros((ENS, 128), f32)
    for c in range(CLASSES):
        values = jnp.concatenate([every[:, s * CLASSES + c, :] for s in range(ND)], axis=0)
        center = jnp.mean(values, axis=0, keepdims=True)
        anomaly = values - center
        upper = anomaly.astype(bf16)
        hi_part[:, c * 128:(c + 1) * 128] = upper
        lo_part[:, c * 128:(c + 1) * 128] = (anomaly - upper.astype(f32)).astype(bf16)
        pull = pull + anomaly * (observed[c:c + 1, :] - center)
    squares = dot32(hi_part[...], hi_part[...], OVER_LAST)
    crossed = dot32(hi_part[...], lo_part[...], OVER_LAST)
    gram[:ENS, :] = squares + (crossed + crossed.T)
    drive_tall = jnp.broadcast_to(jnp.sum(pull, axis=1, keepdims=True), (ENS, ENS))
    gram[ENS:, :] = drive_tall.T[:8, :]

    def gram_copy(k):
        dc, dy = k // ND, k % ND
        return pltpu.make_async_remote_copy(
            src_ref=gram, dst_ref=gram_in.at[k - 1], send_sem=g_send, recv_sem=g_recv,
            device_id=(chip + (core + dc) % 2, (y + dy) % ND), device_id_type=MESH,
        )

    for k in (2, 6, 1, 3, 5, 7, 4):
        gram_copy(k).start()
    send_some(CUTS[3], NM)
    whole_wait(gram_in, g_recv)
    summed = gram[...]
    for k in range(7):
        summed = summed + gram_in[k]
    diagonal = iota((ENS, ENS), 0) == iota((ENS, ENS), 1)
    inverse = spd_inverse(summed[:ENS] + jnp.where(diagonal, float(ENS), 0.0))
    lift = jnp.sum(inverse * summed[ENS:ENS + 1], axis=1, keepdims=True)
    mix_t = (
        float(ENS) * (inverse - jnp.mean(inverse, axis=0, keepdims=True))
        + (lift - jnp.mean(lift, axis=0, keepdims=True))
        + 1.0 / ENS
    )
    upper = mix_t.astype(bf16)
    size = ENS * TILE
    natural = (iota((ENS, ENS), 0) == member_of_slot(iota((ENS, ENS), 1))).astype(bf16)
    mix_hi[...] = dot32(natural, upper).astype(bf16)
    mix_lo[...] = dot32(natural, (mix_t - upper.astype(f32)).astype(bf16)).astype(bf16)

    whole_wait(theta, a_recv)
    is_owner = (me - 3) % 17 == 0
    my_tile = pl.ds(pl.multiple_of(((me + 14) // 17 - 1) % 4 * 128, 128), 128)

    @pl.when(is_owner)
    def _():
        whole_wait(theta_last, l_recv)

    mr, mcol = middle_block(me)
    fr, fcol = first_block(me)

    def results(slot, p, remote):
        jobs = (
            (out.at[pair(slot), :, pl.ds(0, WIDE)], new_middle.at[:, mr, mcol], um_recv),
            (out.at[pair(slot), :, pl.ds(WIDE, SLIM)], new_first.at[:, fr, fcol], uf_recv),
        )
        for src, dst, sem in jobs:
            if remote:
                pltpu.make_async_remote_copy(
                    src_ref=src, dst_ref=dst, send_sem=u_send, recv_sem=sem, device_id=(p, y), device_id_type=MESH
                ).start()
            else:
                pltpu.make_async_copy(src, dst, sem).start()

        @pl.when(is_owner)
        def _():
            src, dst = out_last.at[pair(slot)], new_last.at[:, :, my_tile]
            if remote:
                pltpu.make_async_remote_copy(
                    src_ref=src, dst_ref=dst, send_sem=ul_send, recv_sem=ul_recv, device_id=(p, y), device_id_type=MESH
                ).start()
            else:
                pltpu.make_async_copy(src, dst, ul_recv).start()

    block = 256

    def one_block(b, carry):
        low = (me % 8 + b) % 8
        k = iota((block, ENS), 0) // TILE
        member = ((k // 2) * 8 + low) * 2 + k % 2
        choose = (member == member_of_slot(iota((block, ENS), 1))).astype(bf16)
        repeat = (iota((ENS, size), 0) == iota((ENS, size), 1) // TILE).astype(bf16)
        keep = (iota((block, size), 0) % TILE) == (iota((block, size), 1) % TILE)
        for source, wide in ((mix_hi, wide_hi), (mix_lo, wide_lo)):
            tall = dot32(choose, source[...], OVER_LAST).astype(bf16)
            wide[...] = jnp.where(keep, dot32(tall, repeat), 0.0).astype(bf16)
        flat = theta[...].reshape(size, WIDE + SLIM)
        mixed = dot32(wide_hi[...], flat) + dot32(wide_lo[...], flat)
        here = pl.ds(pl.multiple_of(b * 16, 16), 16)
        out[here] = mixed.astype(bf16).reshape(16, TILE, WIDE + SLIM)

        @pl.when(is_owner)
        def _():
            tiles = theta_last[...].reshape(size, SLIM)
            done = dot32(wide_hi[...], tiles) + dot32(wide_lo[...], tiles)
            out_last[here] = done.astype(bf16).reshape(16, TILE, SLIM)

        def send_result(turn, inner):
            there = (z + swing(turn)) % 8
            p = there * 8 + low
            slot = b * 8 + there

            @pl.when(p != me)
            def _():
                results(slot, p, True)

            @pl.when(p == me)
            def _():
                results(slot, p, False)

            return inner

        lax.fori_loop(0, 8, send_result, 0)
        return carry

    lax.fori_loop(0, 8, one_block, 0)

    for d in range(1, ND):
        x_copy(d).wait_send()
    give_first(True)
    give_middle(True)
    rest = pl.ds(0, ENS - 2)
    whole_wait(theta.at[rest], a_send)
    for t in range(4):
        @pl.when(me != 3 + 17 * t)
        def _():
            whole_wait(last_rows.at[:, :, pl.ds(t * 128, 128)], l_send.at[t])
    whole_wait(part_in.at[pl.ds(0, 7)], p_send)
    whole_wait(every.at[pl.ds(0, 7)], s_send.at[0])
    whole_wait(every.at[pl.ds(0, 24)], s_send.at[1])
    whole_wait(gram_in, g_send)
    whole_wait(new_middle, um_recv)
    whole_wait(new_first, uf_recv)
    whole_wait(new_last, ul_recv)
    whole_wait(out.at[rest], u_send)

    @pl.when(is_owner)
    def _():
        whole_wait(out_last.at[rest], ul_send)


def settle(middle, first, settled_middle, settled_first, held_middle, held_first, in_sems, out_sems):
    steps = []
    for m in range(2):
        for k in range(4):
            at = (m, pl.ds(k * 128, 128))
            steps.append((middle.at[at], held_middle.at[at], settled_middle.at[at], in_sems.at[m, k], out_sems.at[m, k]))
        steps.append((first.at[m], held_first.at[m], settled_first.at[m], in_sems.at[m, 4], out_sems.at[m, 4]))
    ins = [pltpu.make_async_copy(src, held, sem) for src, held, _, sem, _ in steps]
    outs = [pltpu.make_async_copy(held, dst, sem) for _, held, dst, _, sem in steps]
    for copy in ins:
        copy.start()
    for came, goes in zip(ins, outs):
        came.wait()
        goes.start()
    for copy in outs:
        copy.wait()


def on_device(
    feature_pool, labels, sample_rows, noise_variance, first_weight, middle_weight, last_weight
):
    anyspace = pl.BlockSpec(memory_space=pl.ANY)
    vmem = pl.BlockSpec(memory_space=pltpu.VMEM)
    smem = pl.BlockSpec(memory_space=pltpu.SMEM)
    bf16, f32 = jnp.bfloat16, jnp.float32
    dma = pltpu.SemaphoreType.DMA
    new_first, new_middle, new_last = pl.pallas_call(
        kernel,
        out_shape=(
            jax.ShapeDtypeStruct(first_weight.shape, bf16),
            jax.ShapeDtypeStruct(middle_weight.shape, bf16),
            jax.ShapeDtypeStruct((2, TILE, 512), bf16),
        ),
        in_specs=[anyspace, anyspace, vmem, vmem, vmem, vmem, smem],
        out_specs=(anyspace, anyspace, anyspace),
        scratch_shapes=[
            pltpu.VMEM((ENS, TILE, WIDE + SLIM), bf16),
            pltpu.VMEM((ENS, TILE, SLIM), bf16),
            pltpu.VMEM((ND, 256, 512), bf16),
            pltpu.VMEM((2, ND, 512, 512), bf16),
            pltpu.VMEM((ND, 256, 256), bf16),
            pltpu.VMEM((ND, 1024, 512), bf16),
            pltpu.VMEM((1024, 512), f32),
            pltpu.VMEM((2, TILE, 512), bf16),
            pltpu.VMEM((2, TILE, 512), bf16),
            pltpu.VMEM((ND, 2, 16, 128), f32),
            pltpu.VMEM((2 * ND, 16, 128), f32),
            pltpu.VMEM((32, ND * CLASSES, 128), f32),
            pltpu.VMEM((ENS, CLASSES * 128), bf16),
            pltpu.VMEM((ENS, CLASSES * 128), bf16),
            pltpu.VMEM((ENS + 8, ENS), f32),
            pltpu.VMEM((7, ENS + 8, ENS), f32),
            pltpu.VMEM((ENS, ENS), bf16),
            pltpu.VMEM((ENS, ENS), bf16),
            pltpu.VMEM((256, ENS * TILE), bf16),
            pltpu.VMEM((256, ENS * TILE), bf16),
            pltpu.VMEM((ENS, TILE, WIDE + SLIM), bf16),
            pltpu.VMEM((ENS, TILE, SLIM), bf16),
            dma((ND,)), dma((ND,)),
            dma((2, 2)), dma((ND,)),
            dma((2, 2, 2)), dma((2, ND)),
            dma((2,)), dma((2,)),
            dma, dma,
            dma((4,)), dma,
            dma, dma,
            dma((2,)), dma((2,)),
            dma, dma,
            dma, dma, dma, dma, dma,
        ],
        compiler_params=pltpu.CompilerParams(collective_id=0, has_side_effects=True, vmem_limit_bytes=VMEM_LIMIT),
    )(
        first_weight, middle_weight, feature_pool, labels.reshape(1, -1), sample_rows.reshape(1, -1), jnp.transpose(last_weight, (2, 0, 1)),
        noise_variance,
    )
    new_middle, new_first = pl.pallas_call(
        settle,
        out_shape=(
            jax.ShapeDtypeStruct(middle_weight.shape, bf16),
            jax.ShapeDtypeStruct(first_weight.shape, bf16),
        ),
        in_specs=[anyspace, anyspace],
        out_specs=(anyspace, anyspace),
        scratch_shapes=[
            pltpu.VMEM(middle_weight.shape, bf16), pltpu.VMEM(first_weight.shape, bf16), dma((2, 5)), dma((2, 5)),
        ],
        compiler_params=pltpu.CompilerParams(vmem_limit_bytes=VMEM_LIMIT),
    )(new_middle, new_first)
    new_last = jnp.swapaxes(new_last[:, :CLASSES, :], 1, 2)
    return (new_first, new_middle, new_last)


def solution(mesh):
    in_specs = (
        P("dp", None),
        P("dp"),
        P("dp"),
        P(),
        P("member", None, "dp"),
        P("member", "dp", None),
        P("member", "dp", None),
    )
    out_specs = (P("member", None, "dp"), P("member", "dp", None), P("member", "dp", None))
    return jax.shard_map(
        on_device, mesh=mesh, in_specs=in_specs, out_specs=out_specs, check_vma=False
    )
```
